32 devices in a mesh: energy: 8 (over z, x), atom: 4 (over y, core).
Axes of the slice: x: 2, y: 2, z: 4, core: 2. Of those that a mesh axis runs over, the one named last changes fastest.
Arguments:
- green_blocks: float32 [32, 32, 34, 288], P('energy', 'atom'), may hold values from -6 to 6
- coupling: float32 [32, 12, 12], P('atom'), may hold values from -1.75 to 1.75
- neighbours: int32 [32, 34], P('atom'), may hold values from 0 to 31
- freq_offset: int32 [64], replicated, may hold values from 1 to 2, as said below
- emit_weight: float32 [64], replicated, may hold values from 0.02 to 0.2
- absorb_weight: float32 [64], replicated, may hold values from 0.02 to 0.2
Outputs:
- sigma: float32 [32, 32, 34, 288], P('energy', 'atom')
The draws below stay inside these ranges and needn't reach their ends.
Inputs may be any that keep to these rules, and one draw needn't show every extreme that they name: `freq_offset`: every offset is 1 or more and at least one offset equals 2.
All inputs are finite; a program needn't handle non-finite values.
Results may differ from the reference program's by a relative error of at most 0.00007.
Values sent between devices are 32-bit elements; how exact they have to be, the bound alone decides.
A program may use at most 128 MiB of HBM per device.

```python
import math
import jax
import jax.numpy as jnp
from jax import lax

ORB = 12
NBR = 34
NQ = 64
OFF = 2
NE = 32
ATOMS = 32
BLOCK = 288


def draw_freq_offset(key, part):
    values = jax.random.randint(key, (NQ,), 1, OFF + 1).astype(jnp.int32)
    where_top = jax.random.randint(jax.random.fold_in(key, 7), (), 0, NQ)
    return values.at[where_top].set(OFF).astype(jnp.int32)


def place_ends(array, key, low, top_value):
    dims = array.shape
    place = [jax.random.randint(jax.random.fold_in(key, axis), (), 0, dims[axis]) for axis in range(len(dims))]
    array = array.at[tuple(place)].set(low)
    longest = dims.index(max(dims))
    place[longest] = (place[longest] + 1) % dims[longest]
    return array.at[tuple(place)].set(top_value)


def block_scale(rng, shape, split, least, top_value):
    def one(dim, shards_of):
        draws = jax.random.uniform(jax.random.fold_in(jax.random.fold_in(rng, 6), dim), (shards_of,), jnp.float32, least / len(split), top_value / len(split))
        return jnp.repeat(jnp.exp(draws), shape[dim] // shards_of).reshape((-1,) + (1,) * (len(shape) - dim - 1))

    gain = one(*split[0])
    for cut in split[1:]:
        gain = gain * one(*cut)
    return gain


def scatter_about(stream_key, extent, deviation, reach, shards=(), dtype=jnp.bfloat16):
    drawn = jax.random.normal(stream_key, extent, jnp.float32) * deviation
    if len(shards) > 0:
        drawn = block_scale(stream_key, extent, shards, -0.22, 0.18) * drawn
    return jnp.clip(drawn, min=-reach, max=reach).astype(dtype)


def setup_inputs(seed: int = 0) -> dict:
    streams_of = jax.random.split(jax.random.key(seed), 7)
    return {
        "green_blocks": scatter_about(streams_of[0], (NE, ATOMS, NBR, BLOCK), 1.0, 6.0, ((0, 8), (1, 4)), jnp.float32),
        "coupling": scatter_about(streams_of[1], (ATOMS, ORB, ORB), ORB ** -0.5, 1.75, ((0, 4),), jnp.float32),
        "neighbours": place_ends(jax.random.randint(streams_of[2], (ATOMS, NBR), 0, ATOMS), jax.random.fold_in(streams_of[2], 1), 0, ATOMS - 1).astype(jnp.int32),
        "freq_offset": draw_freq_offset(jax.random.fold_in(streams_of[6], 71), 0),
        "emit_weight": jnp.clip(jnp.exp(jax.random.uniform(streams_of[4], (NQ,), jnp.float32, math.log(0.02), math.log(0.2))), 0.02, 0.2),
        "absorb_weight": jnp.clip(jnp.exp(jax.random.uniform(streams_of[5], (NQ,), jnp.float32, math.log(0.02), math.log(0.2))), 0.02, 0.2),
    }


def offset_kernel(freq_offset, emit_weight, absorb_weight):
    shifts = (jnp.arange(2 * OFF + 1) - OFF).astype(jnp.int32)
    emitted = jnp.where(shifts[:, None] == -freq_offset[None, :], emit_weight[None, :], 0.0)
    absorbed = jnp.where(shifts[:, None] == freq_offset[None, :], absorb_weight[None, :], 0.0)
    return jnp.sum(emitted + absorbed, axis=1)


def reference(green_blocks, coupling, neighbours, freq_offset, emit_weight, absorb_weight):
    kernel = offset_kernel(freq_offset, emit_weight, absorb_weight)
    nearby = coupling[neighbours]

    def one_atom(inputs):
        block, left, right = inputs
        parts = block.reshape(NE, NBR, 2, ORB, ORB)
        inner = jnp.einsum("ab,encbd->encad", left, parts, precision=lax.Precision.HIGHEST)
        dressed = jnp.einsum("encad,nfd->encaf", inner, right, precision=lax.Precision.HIGHEST)
        padded = jnp.pad(dressed, ((OFF, OFF), (0, 0), (0, 0), (0, 0), (0, 0)))
        total = jnp.zeros_like(dressed)
        for shift_index in range(2 * OFF + 1):
            total = total + kernel[shift_index] * padded[shift_index:shift_index + NE]
        return total.reshape(NE, NBR, BLOCK)

    result = lax.map(one_atom, (jnp.moveaxis(green_blocks, 1, 0), coupling, nearby))
    return jnp.moveaxis(result, 0, 1)
```

```python
import functools

import jax
import jax.numpy as jnp
from jax import lax
from jax.experimental import pallas as pl
from jax.experimental.pallas import tpu as pltpu
from jax.sharding import PartitionSpec as P

OFF = 2
LANES = 128
MESH = pl.DeviceIdType.MESH


def kernel(
    energy_count,
    atom_count,
    x_ref,
    coup_ref,
    nbr_ref,
    freq_ref,
    emit_ref,
    absorb_ref,
    out_ref,
    gbuf,
    obuf,
    call,
    right_coef,
    left_coef,
    xt,
    mid,
    ot,
    local_sem,
    out_sem,
    halo_send,
    halo_recv,
    coup_send,
    coup_recv,
):
    rows, nbrs, atoms, width = x_ref.shape
    orb = coup_ref.shape[0]
    cells = orb * orb
    per_tile = LANES // atoms
    tiles = -(-nbrs // per_tile)
    spans = [(t * per_tile, min(per_tile, nbrs - t * per_tile)) for t in range(tiles)]
    order = sorted(range(tiles), key=lambda t: (spans[t][1], t))
    all_atoms = atoms * atom_count

    me_e = lax.axis_index("energy")
    me_a = lax.axis_index("atom")
    has_left = me_e > 0
    has_right = me_e < energy_count - 1

    barrier = pltpu.get_barrier_semaphore()

    def greet(e, a):
        pl.semaphore_signal(barrier, inc=1, device_id=(e, a), device_id_type=MESH)

    @pl.when(has_left)
    def _():
        greet(me_e - 1, me_a)

    @pl.when(has_right)
    def _():
        greet(me_e + 1, me_a)

    partners = [lax.rem(me_a + k, atom_count) for k in range(1, atom_count)]
    for partner in partners:
        greet(me_e, partner)
    inner = jnp.logical_and(has_left, has_right)

    @pl.when(inner)
    def _():
        pl.semaphore_wait(barrier, atom_count + 1)

    @pl.when(jnp.logical_not(inner))
    def _():
        pl.semaphore_wait(barrier, atom_count)

    def halo(t, to_right):
        start, count = spans[t]
        src_row, dst_row, side = (rows - OFF, 0, 0) if to_right else (0, rows + OFF, 1)
        return pltpu.make_async_remote_copy(
            src_ref=x_ref.at[pl.ds(src_row, OFF), pl.ds(start, count)],
            dst_ref=gbuf.at[pl.ds(dst_row, OFF), pl.ds(start, count)],
            send_sem=halo_send.at[side, t],
            recv_sem=halo_recv.at[side, t],
            device_id=(me_e + 1 if to_right else me_e - 1, me_a),
            device_id_type=MESH,
        )

    coup_copies = []
    for k, partner in enumerate(partners):
        copy = pltpu.make_async_remote_copy(
            src_ref=coup_ref,
            dst_ref=call.at[:, pl.ds(pl.multiple_of(me_a * atoms, atoms), atoms)],
            send_sem=coup_send.at[k],
            recv_sem=coup_recv.at[k],
            device_id=(me_e, partner),
            device_id_type=MESH,
        )
        copy.start()
        coup_copies.append(copy)

    for t in order:

        @pl.when(has_right)
        def _():
            halo(t, True).start()

        @pl.when(has_left)
        def _():
            halo(t, False).start()

    local = pltpu.make_async_copy(x_ref, gbuf.at[pl.ds(OFF, rows), pl.ds(0, nbrs)], local_sem)
    local.start()

    call[:, pl.ds(pl.multiple_of(me_a * atoms, atoms), atoms), :] = coup_ref[...]

    @pl.when(jnp.logical_not(has_left))
    def _():
        gbuf[0:OFF] = jnp.zeros((OFF,) + gbuf.shape[1:], jnp.float32)

    @pl.when(jnp.logical_not(has_right))
    def _():
        gbuf[rows + OFF : rows + 2 * OFF] = jnp.zeros((OFF,) + gbuf.shape[1:], jnp.float32)

    freq = freq_ref[...]

    def weight(ref, step):
        return jnp.sum(jnp.where(freq == step, ref[...], 0.0), axis=1, keepdims=True)

    weights = [
        (0, weight(emit_ref, 2)),
        (1, weight(emit_ref, 1)),
        (3, weight(absorb_ref, 1)),
        (4, weight(absorb_ref, 2)),
    ]

    lanes = tiles * LANES
    slot = lax.broadcasted_iota(jnp.int32, (nbrs, lanes), 0)
    pair = lax.broadcasted_iota(jnp.int32, (nbrs, lanes), 1)
    spread = jnp.where(pair // atoms == slot, 1.0, 0.0).astype(jnp.float32)
    listed = jnp.dot(
        nbr_ref[...].astype(jnp.float32), spread, preferred_element_type=jnp.float32, precision=lax.Precision.HIGHEST
    )
    atom_row = lax.broadcasted_iota(jnp.int32, (atoms, lanes), 0)
    atom_pair = lax.broadcasted_iota(jnp.int32, (atoms, lanes), 1)
    own = jnp.where(atom_pair % atoms == atom_row, 1.0, 0.0).astype(jnp.float32)
    index = jnp.sum(listed * own, axis=0, keepdims=True)
    ids = lax.broadcasted_iota(jnp.int32, (all_atoms, lanes), 0).astype(jnp.float32)
    chosen = jnp.where(ids == index, 1.0, 0.0).astype(jnp.float32)

    def expand(source, select, target):
        def one(a, carry):
            table = lax.dot_general(
                source[a],
                select,
                (((0,), (0,)), ((), ())),
                preferred_element_type=jnp.float32,
                precision=lax.Precision.HIGHEST,
            )
            for t in range(tiles):
                for d in range(orb):
                    row = table[d : d + 1, t * LANES : (t + 1) * LANES]
                    target[t, a * orb + d] = jnp.broadcast_to(row, (8, LANES))
            return carry

        lax.fori_loop(0, orb, one, 0)

    expand(coup_ref, own, left_coef)
    for copy in coup_copies:
        copy.wait()
    expand(call, chosen, right_coef)
    local.wait()

    outs = []
    for t in order:
        start, count = spans[t]

        @pl.when(has_left)
        def _():
            halo(t, True).wait_recv()

        @pl.when(has_right)
        def _():
            halo(t, False).wait_recv()

        def load(e, carry):
            total = None
            for step, factor in weights:
                term = gbuf[e + step, pl.ds(start, per_tile)].reshape(LANES, width) * factor
                total = term if total is None else total + term
            xt[pl.ds(pl.multiple_of(e * width, 8), width), :] = jnp.transpose(total)
            return carry

        lax.fori_loop(0, rows, load, 0)

        def times_right(b, carry):
            held = jnp.stack([xt[pl.ds(b * orb + d, 8, stride=cells), :] for d in range(orb)])
            for f in range(orb):
                mid[f * orb + b] = jnp.sum(right_coef[t, f * orb : (f + 1) * orb] * held, axis=0)
            return carry

        lax.fori_loop(0, orb, times_right, 0)

        def times_left(f, carry):
            held = mid[pl.ds(f * orb, orb)]
            for a in range(orb):
                ot[pl.ds(a * orb + f, 8, stride=cells), :] = jnp.sum(
                    left_coef[t, a * orb : (a + 1) * orb] * held, axis=0
                )
            return carry

        lax.fori_loop(0, orb, times_left, 0)

        def store(e, carry):
            block = jnp.transpose(ot[pl.ds(pl.multiple_of(e * width, 8), width), :])
            obuf[e, pl.ds(start, per_tile)] = block.reshape(per_tile, atoms, width)
            return carry

        lax.fori_loop(0, rows, store, 0)

        copy = pltpu.make_async_copy(
            obuf.at[:, pl.ds(start, count)], out_ref.at[:, pl.ds(start, count)], out_sem.at[t]
        )
        copy.start()
        outs.append(copy)

    for t in order:

        @pl.when(has_right)
        def _():
            halo(t, True).wait_send()

        @pl.when(has_left)
        def _():
            halo(t, False).wait_send()

    for copy in outs:
        copy.wait()


def local(energy_count, atom_count, green_blocks, coupling, neighbours, freq_offset, emit_weight, absorb_weight):
    rows, atoms, nbrs, width = green_blocks.shape
    orb = coupling.shape[1]
    tiles = -(-(nbrs * atoms) // LANES)
    padded = tiles * LANES // atoms
    vmem = pl.BlockSpec(memory_space=pltpu.VMEM)
    anywhere = pl.BlockSpec(memory_space=pl.ANY)
    f32 = jnp.float32
    result = pl.pallas_call(
        functools.partial(kernel, energy_count, atom_count),
        out_shape=jax.ShapeDtypeStruct((rows, nbrs, atoms, width), f32),
        in_specs=[anywhere, vmem, vmem, vmem, vmem, vmem],
        out_specs=anywhere,
        scratch_shapes=[
            pltpu.VMEM((rows + 2 * OFF, padded, atoms, width), f32),
            pltpu.VMEM((rows, padded, atoms, width), f32),
            pltpu.VMEM((orb, atoms * atom_count, orb), f32),
            pltpu.VMEM((tiles, orb * orb, 8, LANES), f32),
            pltpu.VMEM((tiles, orb * orb, 8, LANES), f32),
            pltpu.VMEM((rows * width, LANES), f32),
            pltpu.VMEM((orb * orb, 8, LANES), f32),
            pltpu.VMEM((rows * width, LANES), f32),
            pltpu.SemaphoreType.DMA,
            pltpu.SemaphoreType.DMA((tiles,)),
            pltpu.SemaphoreType.DMA((2, tiles)),
            pltpu.SemaphoreType.DMA((2, tiles)),
            pltpu.SemaphoreType.DMA((max(atom_count - 1, 1),)),
            pltpu.SemaphoreType.DMA((max(atom_count - 1, 1),)),
        ],
        compiler_params=pltpu.CompilerParams(
            collective_id=0, has_side_effects=True, vmem_limit_bytes=48 * 1024 * 1024
        ),
    )(
        jnp.transpose(green_blocks, (0, 2, 1, 3)),
        jnp.transpose(coupling, (1, 0, 2)),
        neighbours,
        freq_offset.reshape(1, -1),
        emit_weight.reshape(1, -1),
        absorb_weight.reshape(1, -1),
    )
    return jnp.transpose(result, (0, 2, 1, 3))


def solution(mesh):
    placed = (
        P("energy", "atom", None, None),
        P("atom", None, None),
        P("atom", None),
        P(),
        P(),
        P(),
    )
    return jax.shard_map(
        functools.partial(local, mesh.shape["energy"], mesh.shape["atom"]),
        mesh=mesh,
        in_specs=placed,
        out_specs=P("energy", "atom", None, None),
        check_vma=False,
    )
```

```python
import functools

import jax
import jax.numpy as jnp
from jax import lax
from jax.experimental import pallas as pl
from jax.experimental.pallas import tpu as pltpu
from jax.sharding import PartitionSpec as P

OFF = 2
LANES = 128
MESH = pl.DeviceIdType.MESH


def kernel(
    energy_count,
    atom_count,
    x_ref,
    coup_hbm,
    nbr_hbm,
    freq_hbm,
    emit_hbm,
    absorb_hbm,
    out_ref,
    coup_ref,
    nbr_ref,
    freq_ref,
    emit_ref,
    absorb_ref,
    gbuf,
    obuf,
    packed,
    arrived,
    call,
    right_coef,
    left_coef,
    xt,
    mid,
    ot,
    load_sem,
    out_sem,
    halo_send,
    halo_recv,
    coup_send,
    coup_recv,
):
    rows, nbrs, atoms, width = x_ref.shape
    orb = coup_hbm.shape[0]
    cells = orb * orb
    per_tile = LANES // atoms
    tiles = -(-nbrs // per_tile)
    spans = [(t * per_tile, min(per_tile, nbrs - t * per_tile)) for t in range(tiles)]
    order = [0] + sorted(range(1, tiles), key=lambda t: (spans[t][1], t))
    full = width // LANES * LANES
    rest = width - full
    groups = LANES // rest
    all_atoms = atoms * atom_count

    me_e = lax.axis_index("energy")
    me_a = lax.axis_index("atom")
    has_left = me_e > 0
    has_right = me_e < energy_count - 1

    barrier = pltpu.get_barrier_semaphore()

    def greet(e, a):
        pl.semaphore_signal(barrier, inc=1, device_id=(e, a), device_id_type=MESH)

    @pl.when(has_left)
    def _():
        greet(me_e - 1, me_a)

    @pl.when(has_right)
    def _():
        greet(me_e + 1, me_a)

    partners = [lax.rem(me_a + k, atom_count) for k in range(1, atom_count)]
    for partner in partners:
        greet(me_e, partner)
    loads = []
    for k, (src, dst) in enumerate(
        [
            (x_ref, gbuf.at[pl.ds(OFF, rows), pl.ds(0, nbrs)]),
            (coup_hbm, coup_ref),
            (nbr_hbm, nbr_ref),
            (freq_hbm, freq_ref),
            (emit_hbm, emit_ref),
            (absorb_hbm, absorb_ref),
        ]
    ):
        copy = pltpu.make_async_copy(src, dst, load_sem.at[k])
        copy.start()
        loads.append(copy)

    inner = jnp.logical_and(has_left, has_right)

    @pl.when(inner)
    def _():
        pl.semaphore_wait(barrier, atom_count + 1)

    @pl.when(jnp.logical_not(inner))
    def _():
        pl.semaphore_wait(barrier, atom_count)

    def halo(t, to_right):
        src_row, dst_row, side = (rows - OFF, 0, 0) if to_right else (0, rows + OFF, 1)
        if t == tiles:
            src = packed.at[pl.ds(src_row, OFF)]
            dst = arrived.at[pl.ds(side * OFF, OFF)]
        else:
            start, count = spans[t]
            src = x_ref.at[pl.ds(src_row, OFF), pl.ds(start, count), :, pl.ds(0, full)]
            dst = gbuf.at[pl.ds(dst_row, OFF), pl.ds(start, count), :, pl.ds(0, full)]
        return pltpu.make_async_remote_copy(
            src_ref=src,
            dst_ref=dst,
            send_sem=halo_send.at[side, t],
            recv_sem=halo_recv.at[side, t],
            device_id=(me_e + 1 if to_right else me_e - 1, me_a),
            device_id_type=MESH,
        )

    def send(t):
        @pl.when(has_right)
        def _():
            halo(t, True).start()

        @pl.when(has_left)
        def _():
            halo(t, False).start()

    def receive(t):
        @pl.when(has_left)
        def _():
            halo(t, True).wait_recv()

        @pl.when(has_right)
        def _():
            halo(t, False).wait_recv()

    send(order[0])

    coup_copies = []
    for k, partner in enumerate(partners):
        copy = pltpu.make_async_remote_copy(
            src_ref=coup_hbm,
            dst_ref=call.at[:, pl.ds(pl.multiple_of(me_a * atoms, atoms), atoms)],
            send_sem=coup_send.at[k],
            recv_sem=coup_recv.at[k],
            device_id=(me_e, partner),
            device_id_type=MESH,
        )
        copy.start()
        coup_copies.append(copy)

    loads[0].wait()
    gbuf[OFF : OFF + rows, nbrs:] = jnp.zeros((rows, gbuf.shape[1] - nbrs) + gbuf.shape[2:], jnp.float32)

    def pack(m, carry):
        for e in range(rows):
            packed[e, m] = jnp.concatenate(
                [gbuf[OFF + e, m * groups + k, :, full:] for k in range(groups)], axis=-1
            )
        return carry

    lax.fori_loop(0, packed.shape[1], pack, 0)
    send(tiles)
    for t in order[1:]:
        send(t)

    for copy in loads[1:]:
        copy.wait()
    call[:, pl.ds(pl.multiple_of(me_a * atoms, atoms), atoms), :] = coup_ref[...]

    @pl.when(jnp.logical_not(has_left))
    def _():
        gbuf[0:OFF] = jnp.zeros((OFF,) + gbuf.shape[1:], jnp.float32)
        arrived[0:OFF] = jnp.zeros((OFF,) + arrived.shape[1:], jnp.float32)

    @pl.when(jnp.logical_not(has_right))
    def _():
        gbuf[rows + OFF : rows + 2 * OFF] = jnp.zeros((OFF,) + gbuf.shape[1:], jnp.float32)
        arrived[OFF : 2 * OFF] = jnp.zeros((OFF,) + arrived.shape[1:], jnp.float32)

    freq = freq_ref[...]

    def weight(ref, step):
        return jnp.sum(jnp.where(freq == step, ref[...], 0.0), axis=1, keepdims=True)

    weights = [
        (0, weight(emit_ref, 2)),
        (1, weight(emit_ref, 1)),
        (3, weight(absorb_ref, 1)),
        (4, weight(absorb_ref, 2)),
    ]

    lanes = tiles * LANES
    slot = lax.broadcasted_iota(jnp.int32, (nbrs, lanes), 0)
    pair = lax.broadcasted_iota(jnp.int32, (nbrs, lanes), 1)
    spread = jnp.where(pair // atoms == slot, 1.0, 0.0).astype(jnp.float32)
    listed = jnp.dot(
        nbr_ref[...].astype(jnp.float32), spread, preferred_element_type=jnp.float32, precision=lax.Precision.HIGHEST
    )
    atom_row = lax.broadcasted_iota(jnp.int32, (atoms, lanes), 0)
    atom_pair = lax.broadcasted_iota(jnp.int32, (atoms, lanes), 1)
    own = jnp.where(atom_pair % atoms == atom_row, 1.0, 0.0).astype(jnp.float32)
    index = jnp.sum(listed * own, axis=0, keepdims=True)
    ids = lax.broadcasted_iota(jnp.int32, (all_atoms, lanes), 0).astype(jnp.float32)
    chosen = jnp.where(ids == index, 1.0, 0.0).astype(jnp.float32)

    def expand(source, select, target):
        def one(a, carry):
            table = lax.dot_general(
                source[a],
                select,
                (((0,), (0,)), ((), ())),
                preferred_element_type=jnp.float32,
                precision=lax.Precision.HIGHEST,
            )
            for t in range(tiles):
                for d in range(orb):
                    row = table[d : d + 1, t * LANES : (t + 1) * LANES]
                    target[t, a * orb + d] = jnp.broadcast_to(row, (8, LANES))
            return carry

        lax.fori_loop(0, orb, one, 0)

    expand(coup_ref, own, left_coef)
    for copy in coup_copies:
        copy.wait()
    expand(call, chosen, right_coef)

    def unpack(m, carry):
        for row in range(2 * OFF):
            piece = arrived[row, m]
            target = row if row < OFF else rows + row
            for k in range(groups):
                gbuf[target, m * groups + k, :, full:] = piece[:, k * rest : (k + 1) * rest]
        return carry

    outs = []
    for place, t in enumerate(order):
        start, count = spans[t]
        receive(t)
        if place == 0:
            receive(tiles)
            lax.fori_loop(0, packed.shape[1], unpack, 0)

        for e in range(rows):
            total = None
            for step, factor in weights:
                term = gbuf[e + step, pl.ds(start, per_tile)].reshape(LANES, width) * factor
                total = term if total is None else total + term
            xt[e * width : (e + 1) * width, :] = jnp.transpose(total)

        def times_right(pair, carry):
            first = pair * 2
            held = [
                jnp.stack([xt[pl.ds((first + k) * orb + d, 8, stride=cells), :] for d in range(orb)])
                for k in range(2)
            ]
            for f in range(orb):
                factor = right_coef[t, f * orb : (f + 1) * orb]
                for k in range(2):
                    mid[f * orb + first + k] = jnp.sum(factor * held[k], axis=0)
            return carry

        lax.fori_loop(0, orb // 2, times_right, 0)

        def times_left(pair, carry):
            first = pair * 2
            held = [mid[pl.ds((first + k) * orb, orb)] for k in range(2)]
            for a in range(orb):
                factor = left_coef[t, a * orb : (a + 1) * orb]
                for k in range(2):
                    ot[pl.ds(a * orb + first + k, 8, stride=cells), :] = jnp.sum(factor * held[k], axis=0)
            return carry

        lax.fori_loop(0, orb // 2, times_left, 0)

        for e in range(rows):
            block = jnp.transpose(ot[e * width : (e + 1) * width, :])
            obuf[e, start : start + per_tile] = block.reshape(per_tile, atoms, width)
        copy = pltpu.make_async_copy(
            obuf.at[:, pl.ds(start, count)], out_ref.at[:, pl.ds(start, count)], out_sem.at[t]
        )
        copy.start()
        outs.append(copy)

    for t in range(tiles + 1):

        @pl.when(has_right)
        def _():
            halo(t, True).wait_send()

        @pl.when(has_left)
        def _():
            halo(t, False).wait_send()

    for copy in outs:
        copy.wait()


def local(energy_count, atom_count, green_blocks, coupling, neighbours, freq_offset, emit_weight, absorb_weight):
    rows, atoms, nbrs, width = green_blocks.shape
    orb = coupling.shape[1]
    tiles = -(-(nbrs * atoms) // LANES)
    padded = tiles * LANES // atoms
    hbm = pl.BlockSpec(memory_space=pltpu.HBM)
    left_over = LANES // (width % LANES)
    f32 = jnp.float32
    result = pl.pallas_call(
        functools.partial(kernel, energy_count, atom_count),
        out_shape=jax.ShapeDtypeStruct((rows, nbrs, atoms, width), f32),
        in_specs=[hbm] * 6,
        out_specs=hbm,
        scratch_shapes=[
            pltpu.VMEM((orb, atoms, orb), f32),
            pltpu.VMEM((atoms, nbrs), jnp.int32),
            pltpu.VMEM((1, freq_offset.shape[0]), jnp.int32),
            pltpu.VMEM((1, freq_offset.shape[0]), f32),
            pltpu.VMEM((1, freq_offset.shape[0]), f32),
            pltpu.VMEM((rows + 2 * OFF, padded, atoms, width), f32),
            pltpu.VMEM((rows, padded, atoms, width), f32),
            pltpu.VMEM((rows, -(-nbrs // left_over), atoms, LANES), f32),
            pltpu.VMEM((2 * OFF, -(-nbrs // left_over), atoms, LANES), f32),
            pltpu.VMEM((orb, atoms * atom_count, orb), f32),
            pltpu.VMEM((tiles, orb * orb, 8, LANES), f32),
            pltpu.VMEM((tiles, orb * orb, 8, LANES), f32),
            pltpu.VMEM((rows * width, LANES), f32),
            pltpu.VMEM((orb * orb, 8, LANES), f32),
            pltpu.VMEM((rows * width, LANES), f32),
            pltpu.SemaphoreType.DMA((6,)),
            pltpu.SemaphoreType.DMA((tiles,)),
            pltpu.SemaphoreType.DMA((2, tiles + 1)),
            pltpu.SemaphoreType.DMA((2, tiles + 1)),
            pltpu.SemaphoreType.DMA((max(atom_count - 1, 1),)),
            pltpu.SemaphoreType.DMA((max(atom_count - 1, 1),)),
        ],
        compiler_params=pltpu.CompilerParams(
            collective_id=0, has_side_effects=True, vmem_limit_bytes=64 * 1024 * 1024
        ),
    )(
        jnp.transpose(green_blocks, (0, 2, 1, 3)),
        jnp.transpose(coupling, (1, 0, 2)),
        neighbours,
        freq_offset.reshape(1, -1),
        emit_weight.reshape(1, -1),
        absorb_weight.reshape(1, -1),
    )
    return jnp.transpose(result, (0, 2, 1, 3))


def solution(mesh):
    placed = (
        P("energy", "atom", None, None),
        P("atom", None, None),
        P("atom", None),
        P(),
        P(),
        P(),
    )
    return jax.shard_map(
        functools.partial(local, mesh.shape["energy"], mesh.shape["atom"]),
        mesh=mesh,
        in_specs=placed,
        out_specs=P("energy", "atom", None, None),
        check_vma=False,
    )
```

```python
import functools

import jax
import jax.numpy as jnp
from jax import lax
from jax.experimental import pallas as pl
from jax.experimental.pallas import tpu as pltpu
from jax.sharding import PartitionSpec as P

OFF = 2
RELAYED = 3
LANES = 128
MESH = pl.DeviceIdType.MESH


def kernel(
    energy_count,
    atom_count,
    x_ref,
    coup_hbm,
    nbr_hbm,
    freq_hbm,
    emit_hbm,
    absorb_hbm,
    out_ref,
    coup_ref,
    nbr_ref,
    freq_ref,
    emit_ref,
    absorb_ref,
    gbuf,
    packed,
    arrived,
    relay,
    call,
    right_coef,
    left_coef,
    xt,
    mid,
    ot,
    load_sem,
    halo_send,
    halo_recv,
    relay_send,
    relay_recv,
    coup_send,
    coup_recv,
):
    rows, nbrs, atoms, width = x_ref.shape
    orb = coup_hbm.shape[0]
    cells = orb * orb
    per_tile = LANES // atoms
    tiles = -(-nbrs // per_tile)
    spans = [(t * per_tile, min(per_tile, nbrs - t * per_tile)) for t in range(tiles)]
    order = [0] + sorted(range(1, tiles), key=lambda t: (spans[t][1], t))
    full = width // LANES * LANES
    rest = width - full
    groups = LANES // rest
    all_atoms = atoms * atom_count
    half = per_tile // 2
    pieces = [(start, min(half, nbrs - start)) for start in range(0, nbrs, half)]
    held_by = {t: [p for p, (start, _) in enumerate(pieces) if start // per_tile == t] for t in range(tiles)}

    me_e = lax.axis_index("energy")
    me_a = lax.axis_index("atom")
    has_left = me_e > 0
    has_right = me_e < energy_count - 1

    barrier = pltpu.get_barrier_semaphore()

    def greet(e, a):
        pl.semaphore_signal(barrier, inc=1, device_id=(e, a), device_id_type=MESH)

    @pl.when(has_left)
    def _():
        greet(me_e - 1, me_a)

    @pl.when(has_right)
    def _():
        greet(me_e + 1, me_a)

    @pl.when(me_e > 1)
    def _():
        greet(me_e - 2, me_a)

    @pl.when(me_e < energy_count - 2)
    def _():
        greet(me_e + 2, me_a)

    partners = [lax.rem(me_a + k, atom_count) for k in range(1, atom_count)]
    for partner in partners:
        greet(me_e, partner)
    loads = []
    for k, (src, dst) in enumerate(
        [
            (x_ref, gbuf.at[pl.ds(OFF, rows), pl.ds(0, nbrs)]),
            (coup_hbm, coup_ref),
            (nbr_hbm, nbr_ref),
            (freq_hbm, freq_ref),
            (emit_hbm, emit_ref),
            (absorb_hbm, absorb_ref),
        ]
    ):
        copy = pltpu.make_async_copy(src, dst, load_sem.at[k])
        copy.start()
        loads.append(copy)

    outer = jnp.logical_or(me_e == 0, me_e == energy_count - 1)
    beside = jnp.logical_or(me_e == 1, me_e == energy_count - 2)

    @pl.when(outer)
    def _():
        pl.semaphore_wait(barrier, atom_count + 1)

    @pl.when(beside)
    def _():
        pl.semaphore_wait(barrier, atom_count + 2)

    @pl.when(jnp.logical_not(jnp.logical_or(outer, beside)))
    def _():
        pl.semaphore_wait(barrier, atom_count + 3)

    def halo(p, to_right):
        src_row, dst_row, side = (rows - OFF, 0, 0) if to_right else (0, rows + OFF, 1)
        if p == len(pieces):
            src = packed.at[pl.ds(src_row, OFF)]
            dst = arrived.at[pl.ds(side * OFF, OFF)]
        else:
            start, count = pieces[p]
            src = x_ref.at[pl.ds(src_row, OFF), pl.ds(start, count), :, pl.ds(0, full)]
            dst = gbuf.at[pl.ds(dst_row, OFF), pl.ds(start, count), :, pl.ds(0, full)]
        return pltpu.make_async_remote_copy(
            src_ref=src,
            dst_ref=dst,
            send_sem=halo_send.at[side, p],
            recv_sem=halo_recv.at[side, p],
            device_id=(me_e + 1 if to_right else me_e - 1, me_a),
            device_id_type=MESH,
        )

    pairs = energy_count // 2
    mine = lax.div(me_e, 2)
    odd = lax.rem(me_e, 2) == 1
    even = lax.rem(me_e, 2) == 0
    via_right = lax.div((RELAYED + 1) * (pairs - 1 - mine), pairs)
    via_left = lax.div((RELAYED + 1) * mine, pairs)

    def detour(p, to_right):
        start, count = pieces[p]
        src_row, side = (rows - OFF, 0) if to_right else (0, 1)
        return pltpu.make_async_remote_copy(
            src_ref=x_ref.at[pl.ds(src_row, OFF), pl.ds(start, count), :, pl.ds(0, full)],
            dst_ref=relay.at[p],
            send_sem=halo_send.at[side, p],
            recv_sem=relay_recv.at[p],
            device_id=(me_e - 1 if to_right else me_e + 1, me_a),
            device_id_type=MESH,
        )

    def passed_on(p, to_right):
        start, count = pieces[p]
        dst_row, side = (0, 0) if to_right else (rows + OFF, 1)
        return pltpu.make_async_remote_copy(
            src_ref=relay.at[p],
            dst_ref=gbuf.at[pl.ds(dst_row, OFF), pl.ds(start, count), :, pl.ds(0, full)],
            send_sem=relay_send.at[p],
            recv_sem=halo_recv.at[side, p],
            device_id=(me_e + 2 if to_right else me_e - 2, me_a),
            device_id_type=MESH,
        )

    def send(p):
        if p < RELAYED:
            around_right = jnp.logical_and(odd, p < via_right)
            around_left = jnp.logical_and(even, p < via_left)

            @pl.when(around_right)
            def _():
                detour(p, True).start()

            @pl.when(around_left)
            def _():
                detour(p, False).start()

            straight_right = jnp.logical_and(has_right, jnp.logical_not(around_right))
            straight_left = jnp.logical_and(has_left, jnp.logical_not(around_left))
        else:
            straight_right, straight_left = has_right, has_left

        @pl.when(straight_right)
        def _():
            halo(p, True).start()

        @pl.when(straight_left)
        def _():
            halo(p, False).start()

    def forward(p):
        @pl.when(jnp.logical_and(odd, p < via_left))
        def _():
            detour(p, False).wait_recv()
            passed_on(p, False).start()

        @pl.when(jnp.logical_and(even, p < via_right))
        def _():
            detour(p, True).wait_recv()
            passed_on(p, True).start()

    def receive(p):
        @pl.when(has_left)
        def _():
            halo(p, True).wait_recv()

        @pl.when(has_right)
        def _():
            halo(p, False).wait_recv()

    for p in held_by[order[0]]:
        send(p)

    coup_copies = []
    for k, partner in enumerate(partners):
        copy = pltpu.make_async_remote_copy(
            src_ref=coup_hbm,
            dst_ref=call.at[:, pl.ds(pl.multiple_of(me_a * atoms, atoms), atoms)],
            send_sem=coup_send.at[k],
            recv_sem=coup_recv.at[k],
            device_id=(me_e, partner),
            device_id_type=MESH,
        )
        copy.start()
        coup_copies.append(copy)

    loads[0].wait()
    gbuf[OFF : OFF + rows, nbrs:] = jnp.zeros((rows, gbuf.shape[1] - nbrs) + gbuf.shape[2:], jnp.float32)

    def pack(m, carry):
        for e in range(rows):
            packed[e, m] = jnp.concatenate(
                [gbuf[OFF + e, m * groups + k, :, full:] for k in range(groups)], axis=-1
            )
        return carry

    lax.fori_loop(0, packed.shape[1], pack, 0)
    send(len(pieces))
    for t in order[1:]:
        for p in held_by[t]:
            send(p)

    for copy in loads[1:]:
        copy.wait()
    call[:, pl.ds(pl.multiple_of(me_a * atoms, atoms), atoms), :] = coup_ref[...]

    @pl.when(jnp.logical_not(has_left))
    def _():
        gbuf[0:OFF] = jnp.zeros((OFF,) + gbuf.shape[1:], jnp.float32)
        arrived[0:OFF] = jnp.zeros((OFF,) + arrived.shape[1:], jnp.float32)

    @pl.when(jnp.logical_not(has_right))
    def _():
        gbuf[rows + OFF : rows + 2 * OFF] = jnp.zeros((OFF,) + gbuf.shape[1:], jnp.float32)
        arrived[OFF : 2 * OFF] = jnp.zeros((OFF,) + arrived.shape[1:], jnp.float32)

    freq = freq_ref[...]

    def weight(ref, step):
        return jnp.sum(jnp.where(freq == step, ref[...], 0.0), axis=1, keepdims=True)

    weights = [
        (0, weight(emit_ref, 2)),
        (1, weight(emit_ref, 1)),
        (3, weight(absorb_ref, 1)),
        (4, weight(absorb_ref, 2)),
    ]

    lanes = tiles * LANES
    slot = lax.broadcasted_iota(jnp.int32, (nbrs, lanes), 0)
    pair = lax.broadcasted_iota(jnp.int32, (nbrs, lanes), 1)
    spread = jnp.where(pair // atoms == slot, 1.0, 0.0).astype(jnp.float32)
    listed = jnp.dot(
        nbr_ref[...].astype(jnp.float32), spread, preferred_element_type=jnp.float32, precision=lax.Precision.HIGHEST
    )
    atom_row = lax.broadcasted_iota(jnp.int32, (atoms, lanes), 0)
    atom_pair = lax.broadcasted_iota(jnp.int32, (atoms, lanes), 1)
    own = jnp.where(atom_pair % atoms == atom_row, 1.0, 0.0).astype(jnp.float32)
    index = jnp.sum(listed * own, axis=0, keepdims=True)
    ids = lax.broadcasted_iota(jnp.int32, (all_atoms, lanes), 0).astype(jnp.float32)
    chosen = jnp.where(ids == index, 1.0, 0.0).astype(jnp.float32)

    def expand(source, select, target):
        def one(a, carry):
            table = lax.dot_general(
                source[a],
                select,
                (((0,), (0,)), ((), ())),
                preferred_element_type=jnp.float32,
                precision=lax.Precision.HIGHEST,
            )
            for t in range(tiles):
                for d in range(orb):
                    row = table[d : d + 1, t * LANES : (t + 1) * LANES]
                    target[t, a * orb + d] = jnp.broadcast_to(row, (8, LANES))
            return carry

        lax.fori_loop(0, orb, one, 0)

    expand(coup_ref, own, left_coef)
    forward(0)
    for copy in coup_copies:
        copy.wait()
    expand(call, chosen, right_coef)
    for p in range(1, RELAYED - 1):
        forward(p)

    def unpack(m, carry):
        for row in range(2 * OFF):
            piece = arrived[row, m]
            target = row if row < OFF else rows + row
            for k in range(groups):
                gbuf[target, m * groups + k, :, full:] = piece[:, k * rest : (k + 1) * rest]
        return carry

    for place, t in enumerate(order):
        start, count = spans[t]
        if place == 1:
            forward(RELAYED - 1)
        for p in held_by[t]:
            receive(p)
        if place == 0:
            receive(len(pieces))
            lax.fori_loop(0, packed.shape[1], unpack, 0)

        for e in range(rows):
            total = None
            for step, factor in weights:
                term = gbuf[e + step, pl.ds(start, per_tile)].reshape(LANES, width) * factor
                total = term if total is None else total + term
            xt[e * width : (e + 1) * width, :] = jnp.transpose(total)

        def times_right(pair, carry):
            first = pair * 2
            held = [
                jnp.stack([xt[pl.ds((first + k) * orb + d, 8, stride=cells), :] for d in range(orb)])
                for k in range(2)
            ]
            for f in range(orb):
                factor = right_coef[t, f * orb : (f + 1) * orb]
                for k in range(2):
                    mid[f * orb + first + k] = jnp.sum(factor * held[k], axis=0)
            return carry

        lax.fori_loop(0, orb // 2, times_right, 0)

        def times_left(pair, carry):
            first = pair * 2
            held = [mid[pl.ds((first + k) * orb, orb)] for k in range(2)]
            for a in range(orb):
                factor = left_coef[t, a * orb : (a + 1) * orb]
                for k in range(2):
                    ot[pl.ds(a * orb + first + k, 8, stride=cells), :] = jnp.sum(factor * held[k], axis=0)
            return carry

        lax.fori_loop(0, orb // 2, times_left, 0)

        for e in range(rows):
            block = jnp.transpose(ot[e * width : (e + 1) * width, :])
            out_ref[e, start : start + count] = block[: count * atoms].reshape(count, atoms, width)

    for p in range(len(pieces) + 1):

        @pl.when(has_right)
        def _():
            halo(p, True).wait_send()

        @pl.when(has_left)
        def _():
            halo(p, False).wait_send()

    for p in range(RELAYED):

        @pl.when(jnp.logical_and(odd, p < via_left))
        def _():
            passed_on(p, False).wait_send()

        @pl.when(jnp.logical_and(even, p < via_right))
        def _():
            passed_on(p, True).wait_send()


def local(energy_count, atom_count, green_blocks, coupling, neighbours, freq_offset, emit_weight, absorb_weight):
    rows, atoms, nbrs, width = green_blocks.shape
    orb = coupling.shape[1]
    tiles = -(-(nbrs * atoms) // LANES)
    padded = tiles * LANES // atoms
    hbm = pl.BlockSpec(memory_space=pltpu.HBM)
    piece_count = -(-nbrs // (LANES // atoms // 2))
    left_over = LANES // (width % LANES)
    f32 = jnp.float32
    result = pl.pallas_call(
        functools.partial(kernel, energy_count, atom_count),
        out_shape=pltpu.VMEM((rows, nbrs, atoms, width), f32),
        in_specs=[hbm] * 6,
        out_specs=pl.BlockSpec(memory_space=pltpu.VMEM),
        scratch_shapes=[
            pltpu.VMEM((orb, atoms, orb), f32),
            pltpu.VMEM((atoms, nbrs), jnp.int32),
            pltpu.VMEM((1, freq_offset.shape[0]), jnp.int32),
            pltpu.VMEM((1, freq_offset.shape[0]), f32),
            pltpu.VMEM((1, freq_offset.shape[0]), f32),
            pltpu.VMEM((rows + 2 * OFF, padded, atoms, width), f32),
            pltpu.VMEM((rows, -(-nbrs // left_over), atoms, LANES), f32),
            pltpu.VMEM((2 * OFF, -(-nbrs // left_over), atoms, LANES), f32),
            pltpu.VMEM((RELAYED, OFF, LANES // atoms // 2, atoms, width // LANES * LANES), f32),
            pltpu.VMEM((orb, atoms * atom_count, orb), f32),
            pltpu.VMEM((tiles, orb * orb, 8, LANES), f32),
            pltpu.VMEM((tiles, orb * orb, 8, LANES), f32),
            pltpu.VMEM((rows * width, LANES), f32),
            pltpu.VMEM((orb * orb, 8, LANES), f32),
            pltpu.VMEM((rows * width, LANES), f32),
            pltpu.SemaphoreType.DMA((6,)),
            pltpu.SemaphoreType.DMA((2, piece_count + 1)),
            pltpu.SemaphoreType.DMA((2, piece_count + 1)),
            pltpu.SemaphoreType.DMA((RELAYED,)),
            pltpu.SemaphoreType.DMA((RELAYED,)),
            pltpu.SemaphoreType.DMA((max(atom_count - 1, 1),)),
            pltpu.SemaphoreType.DMA((max(atom_count - 1, 1),)),
        ],
        compiler_params=pltpu.CompilerParams(
            collective_id=0, has_side_effects=True, vmem_limit_bytes=48 * 1024 * 1024
        ),
    )(
        *(
            pltpu.with_memory_space_constraint(operand, pltpu.HBM)
            for operand in (
                jnp.transpose(green_blocks, (0, 2, 1, 3)),
                jnp.transpose(coupling, (1, 0, 2)),
                neighbours,
                freq_offset.reshape(1, -1),
                emit_weight.reshape(1, -1),
                absorb_weight.reshape(1, -1),
            )
        )
    )
    return jnp.transpose(result, (0, 2, 1, 3))


def solution(mesh):
    placed = (
        P("energy", "atom", None, None),
        P("atom", None, None),
        P("atom", None),
        P(),
        P(),
        P(),
    )
    return jax.shard_map(
        functools.partial(local, mesh.shape["energy"], mesh.shape["atom"]),
        mesh=mesh,
        in_specs=placed,
        out_specs=P("energy", "atom", None, None),
        check_vma=False,
    )
```

```python
import functools

import jax
import jax.numpy as jnp
from jax import lax
from jax.experimental import pallas as pl
from jax.experimental.pallas import tpu as pltpu
from jax.sharding import PartitionSpec as P

OFF = 2
RELAYED = 3
LANES = 128
MESH = pl.DeviceIdType.MESH


def kernel(
    energy_count,
    atom_count,
    x_ref,
    coup_hbm,
    nbr_hbm,
    freq_hbm,
    emit_hbm,
    absorb_hbm,
    out_ref,
    coup_ref,
    nbr_ref,
    freq_ref,
    emit_ref,
    absorb_ref,
    gbuf,
    packed,
    arrived,
    relay,
    call,
    right_coef,
    left_coef,
    xt,
    mid,
    ot,
    load_sem,
    halo_send,
    halo_recv,
    relay_send,
    relay_recv,
    coup_send,
    coup_recv,
):
    rows, nbrs, atoms, width = x_ref.shape
    orb = coup_hbm.shape[0]
    cells = orb * orb
    per_tile = LANES // atoms
    tiles = -(-nbrs // per_tile)
    spans = [(t * per_tile, min(per_tile, nbrs - t * per_tile)) for t in range(tiles)]
    full = width // LANES * LANES
    rest = width - full
    groups = LANES // rest
    packs = [(t * per_tile // groups, -(-(spans[t][0] + spans[t][1]) // groups) - t * per_tile // groups) for t in range(tiles)]
    all_atoms = atoms * atom_count
    half = per_tile // 2
    pieces = [(start, min(half, nbrs - start)) for start in range(0, nbrs, half)]
    held_by = {t: [p for p, (start, _) in enumerate(pieces) if start // per_tile == t] for t in range(tiles)}

    me_e = lax.axis_index("energy")
    me_a = lax.axis_index("atom")
    has_left = me_e > 0
    has_right = me_e < energy_count - 1

    barrier = pltpu.get_barrier_semaphore()

    def greet(e, a):
        pl.semaphore_signal(barrier, inc=1, device_id=(e, a), device_id_type=MESH)

    @pl.when(has_left)
    def _():
        greet(me_e - 1, me_a)

    @pl.when(has_right)
    def _():
        greet(me_e + 1, me_a)

    @pl.when(me_e > 1)
    def _():
        greet(me_e - 2, me_a)

    @pl.when(me_e < energy_count - 2)
    def _():
        greet(me_e + 2, me_a)

    partners = [lax.rem(me_a + k, atom_count) for k in range(1, atom_count)]
    for partner in partners:
        greet(me_e, partner)
    loads = []
    for k, (src, dst) in enumerate(
        [
            (x_ref, gbuf.at[pl.ds(OFF, rows), pl.ds(0, nbrs)]),
            (coup_hbm, coup_ref),
            (nbr_hbm, nbr_ref),
            (freq_hbm, freq_ref),
            (emit_hbm, emit_ref),
            (absorb_hbm, absorb_ref),
        ]
    ):
        copy = pltpu.make_async_copy(src, dst, load_sem.at[k])
        copy.start()
        loads.append(copy)

    outer = jnp.logical_or(me_e == 0, me_e == energy_count - 1)
    beside = jnp.logical_or(me_e == 1, me_e == energy_count - 2)

    @pl.when(outer)
    def _():
        pl.semaphore_wait(barrier, atom_count + 1)

    @pl.when(beside)
    def _():
        pl.semaphore_wait(barrier, atom_count + 2)

    @pl.when(jnp.logical_not(jnp.logical_or(outer, beside)))
    def _():
        pl.semaphore_wait(barrier, atom_count + 3)

    def own_rows(p, row):
        start, count = pieces[p]
        ref, row = (x_ref, row) if start < per_tile else (gbuf, row + OFF)
        return ref.at[pl.ds(row, OFF), pl.ds(start, count), :, pl.ds(0, full)]

    def halo(p, to_right):
        src_row, dst_row, side = (rows - OFF, 0, 0) if to_right else (0, rows + OFF, 1)
        if p >= len(pieces):
            first, count = packs[p - len(pieces)]
            src = packed.at[pl.ds(src_row, OFF), pl.ds(first, count)]
            dst = arrived.at[pl.ds(side * OFF, OFF), pl.ds(first, count)]
        else:
            start, count = pieces[p]
            src = own_rows(p, src_row)
            dst = gbuf.at[pl.ds(dst_row, OFF), pl.ds(start, count), :, pl.ds(0, full)]
        return pltpu.make_async_remote_copy(
            src_ref=src,
            dst_ref=dst,
            send_sem=halo_send.at[side, p],
            recv_sem=halo_recv.at[side, p],
            device_id=(me_e + 1 if to_right else me_e - 1, me_a),
            device_id_type=MESH,
        )

    pairs = energy_count // 2
    mine = lax.div(me_e, 2)
    odd = lax.rem(me_e, 2) == 1
    even = lax.rem(me_e, 2) == 0
    via_right = lax.div((RELAYED + 1) * (pairs - 1 - mine), pairs)
    via_left = lax.div((RELAYED + 1) * mine, pairs)

    def detour(p, to_right):
        src_row, side = (rows - OFF, 0) if to_right else (0, 1)
        return pltpu.make_async_remote_copy(
            src_ref=own_rows(p, src_row),
            dst_ref=relay.at[p],
            send_sem=halo_send.at[side, p],
            recv_sem=relay_recv.at[p],
            device_id=(me_e - 1 if to_right else me_e + 1, me_a),
            device_id_type=MESH,
        )

    def passed_on(p, to_right):
        start, count = pieces[p]
        dst_row, side = (0, 0) if to_right else (rows + OFF, 1)
        return pltpu.make_async_remote_copy(
            src_ref=relay.at[p],
            dst_ref=gbuf.at[pl.ds(dst_row, OFF), pl.ds(start, count), :, pl.ds(0, full)],
            send_sem=relay_send.at[p],
            recv_sem=halo_recv.at[side, p],
            device_id=(me_e + 2 if to_right else me_e - 2, me_a),
            device_id_type=MESH,
        )

    def send(p):
        if p < RELAYED:
            around_right = jnp.logical_and(odd, p < via_right)
            around_left = jnp.logical_and(even, p < via_left)

            @pl.when(around_right)
            def _():
                detour(p, True).start()

            @pl.when(around_left)
            def _():
                detour(p, False).start()

            straight_right = jnp.logical_and(has_right, jnp.logical_not(around_right))
            straight_left = jnp.logical_and(has_left, jnp.logical_not(around_left))
        else:
            straight_right, straight_left = has_right, has_left

        @pl.when(straight_right)
        def _():
            halo(p, True).start()

        @pl.when(straight_left)
        def _():
            halo(p, False).start()

    def forward(p):
        @pl.when(jnp.logical_and(odd, p < via_left))
        def _():
            detour(p, False).wait_recv()
            passed_on(p, False).start()

        @pl.when(jnp.logical_and(even, p < via_right))
        def _():
            detour(p, True).wait_recv()
            passed_on(p, True).start()

    def receive(p):
        @pl.when(has_left)
        def _():
            halo(p, True).wait_recv()

        @pl.when(has_right)
        def _():
            halo(p, False).wait_recv()

    for p in held_by[0]:
        send(p)

    coup_copies = []
    for k, partner in enumerate(partners):
        copy = pltpu.make_async_remote_copy(
            src_ref=coup_hbm,
            dst_ref=call.at[:, pl.ds(pl.multiple_of(me_a * atoms, atoms), atoms)],
            send_sem=coup_send.at[k],
            recv_sem=coup_recv.at[k],
            device_id=(me_e, partner),
            device_id_type=MESH,
        )
        copy.start()
        coup_copies.append(copy)

    loads[0].wait()
    gbuf[OFF : OFF + rows, nbrs:] = jnp.zeros((rows, gbuf.shape[1] - nbrs) + gbuf.shape[2:], jnp.float32)

    def send_packed(t):
        first, count = packs[t]

        def pack(m, carry):
            for e in range(rows):
                packed[e, m] = jnp.concatenate(
                    [gbuf[OFF + e, m * groups + k, :, full:] for k in range(groups)], axis=-1
                )
            return carry

        lax.fori_loop(first, first + count, pack, 0)
        send(len(pieces) + t)

    send_packed(0)

    for copy in loads[1:]:
        copy.wait()
    call[:, pl.ds(pl.multiple_of(me_a * atoms, atoms), atoms), :] = coup_ref[...]

    @pl.when(jnp.logical_not(has_left))
    def _():
        gbuf[0:OFF] = jnp.zeros((OFF,) + gbuf.shape[1:], jnp.float32)
        arrived[0:OFF] = jnp.zeros((OFF,) + arrived.shape[1:], jnp.float32)

    @pl.when(jnp.logical_not(has_right))
    def _():
        gbuf[rows + OFF : rows + 2 * OFF] = jnp.zeros((OFF,) + gbuf.shape[1:], jnp.float32)
        arrived[OFF : 2 * OFF] = jnp.zeros((OFF,) + arrived.shape[1:], jnp.float32)

    freq = freq_ref[...]

    def weight(ref, step):
        return jnp.sum(jnp.where(freq == step, ref[...], 0.0), axis=1, keepdims=True)

    weights = [
        (0, weight(emit_ref, 2)),
        (1, weight(emit_ref, 1)),
        (3, weight(absorb_ref, 1)),
        (4, weight(absorb_ref, 2)),
    ]

    lanes = tiles * LANES
    slot = lax.broadcasted_iota(jnp.int32, (nbrs, lanes), 0)
    pair = lax.broadcasted_iota(jnp.int32, (nbrs, lanes), 1)
    spread = jnp.where(pair // atoms == slot, 1.0, 0.0).astype(jnp.float32)
    listed = jnp.dot(
        nbr_ref[...].astype(jnp.float32), spread, preferred_element_type=jnp.float32, precision=lax.Precision.HIGHEST
    )
    atom_row = lax.broadcasted_iota(jnp.int32, (atoms, lanes), 0)
    atom_pair = lax.broadcasted_iota(jnp.int32, (atoms, lanes), 1)
    own = jnp.where(atom_pair % atoms == atom_row, 1.0, 0.0).astype(jnp.float32)
    index = jnp.sum(listed * own, axis=0, keepdims=True)
    ids = lax.broadcasted_iota(jnp.int32, (all_atoms, lanes), 0).astype(jnp.float32)
    chosen = jnp.where(ids == index, 1.0, 0.0).astype(jnp.float32)

    def expand(source, select, target):
        def one(a, carry):
            table = lax.dot_general(
                source[a],
                select,
                (((0,), (0,)), ((), ())),
                preferred_element_type=jnp.float32,
                precision=lax.Precision.HIGHEST,
            )
            for t in range(tiles):
                for d in range(orb):
                    row = table[d : d + 1, t * LANES : (t + 1) * LANES]
                    target[t, a * orb + d] = jnp.broadcast_to(row, (8, LANES))
            return carry

        lax.fori_loop(0, orb, one, 0, unroll=4)

    expand(coup_ref, own, left_coef)
    for copy in coup_copies:
        copy.wait()
    expand(call, chosen, right_coef)

    def dress(t, read, write):
        for e in range(rows):
            xt[e * width : (e + 1) * width, :] = jnp.transpose(read(e))

        def times_right(pair, carry):
            first = pair * 2
            held = [
                jnp.stack([xt[pl.ds((first + k) * orb + d, 8, stride=cells), :] for d in range(orb)])
                for k in range(2)
            ]
            for f in range(orb):
                factor = right_coef[t, f * orb : (f + 1) * orb]
                for k in range(2):
                    mid[f * orb + first + k] = jnp.sum(factor * held[k], axis=0)
            return carry

        lax.fori_loop(0, orb // 2, times_right, 0)

        def times_left(pair, carry):
            first = pair * 2
            held = [mid[pl.ds((first + k) * orb, orb)] for k in range(2)]
            for a in range(orb):
                factor = left_coef[t, a * orb : (a + 1) * orb]
                for k in range(2):
                    ot[pl.ds(a * orb + first + k, 8, stride=cells), :] = jnp.sum(factor * held[k], axis=0)
            return carry

        lax.fori_loop(0, orb // 2, times_left, 0)

        for e in range(rows):
            write(e, jnp.transpose(ot[e * width : (e + 1) * width, :]))

    def filtered(e, start, count):
        total = None
        for step, factor in weights:
            term = gbuf[e + step, pl.ds(start, count)].reshape(count * atoms, width) * factor
            total = term if total is None else total + term
        return total

    def receive_packed(t):
        first, count = packs[t]
        receive(len(pieces) + t)

        def unpack(m, carry):
            for row in range(2 * OFF):
                piece = arrived[row, m]
                target = row if row < OFF else rows + row
                for k in range(groups):
                    gbuf[target, m * groups + k, :, full:] = piece[:, k * rest : (k + 1) * rest]
            return carry

        lax.fori_loop(first, first + count, unpack, 0)

    for t in range(1, tiles):
        start, count = spans[t]

        def write(e, block):
            gbuf[OFF + e, start : start + per_tile] = block.reshape(per_tile, atoms, width)

        dress(t, lambda e: gbuf[OFF + e, start : start + per_tile].reshape(LANES, width), write)
        for p in held_by[t]:
            send(p)
        send_packed(t)
        forward(t - 1)

    for p in range(tiles - 1, RELAYED - 1):
        forward(p)
    for p in held_by[0]:
        receive(p)
    receive_packed(0)

    def write_first(e, block):
        count = spans[0][1]
        out_ref[e, :count] = block[: count * atoms].reshape(count, atoms, width)

    dress(0, lambda e: filtered(e, 0, per_tile), write_first)
    forward(RELAYED - 1)

    for t in range(1, tiles):
        receive_packed(t)
        for p in held_by[t]:
            start, count = pieces[p]
            receive(p)
            for e in range(rows):
                out_ref[e, start : start + count] = filtered(e, start, count).reshape(count, atoms, width)

    for p in range(len(pieces) + tiles):

        @pl.when(has_right)
        def _():
            halo(p, True).wait_send()

        @pl.when(has_left)
        def _():
            halo(p, False).wait_send()

    for p in range(RELAYED):

        @pl.when(jnp.logical_and(odd, p < via_left))
        def _():
            passed_on(p, False).wait_send()

        @pl.when(jnp.logical_and(even, p < via_right))
        def _():
            passed_on(p, True).wait_send()


def local(energy_count, atom_count, green_blocks, coupling, neighbours, freq_offset, emit_weight, absorb_weight):
    rows, atoms, nbrs, width = green_blocks.shape
    orb = coupling.shape[1]
    tiles = -(-(nbrs * atoms) // LANES)
    padded = tiles * LANES // atoms
    hbm = pl.BlockSpec(memory_space=pltpu.HBM)
    piece_count = -(-nbrs // (LANES // atoms // 2))
    left_over = LANES // (width % LANES)
    f32 = jnp.float32
    result = pl.pallas_call(
        functools.partial(kernel, energy_count, atom_count),
        out_shape=pltpu.VMEM((rows, nbrs, atoms, width), f32),
        in_specs=[hbm] * 6,
        out_specs=pl.BlockSpec(memory_space=pltpu.VMEM),
        scratch_shapes=[
            pltpu.VMEM((orb, atoms, orb), f32),
            pltpu.VMEM((atoms, nbrs), jnp.int32),
            pltpu.VMEM((1, freq_offset.shape[0]), jnp.int32),
            pltpu.VMEM((1, freq_offset.shape[0]), f32),
            pltpu.VMEM((1, freq_offset.shape[0]), f32),
            pltpu.VMEM((rows + 2 * OFF, padded, atoms, width), f32),
            pltpu.VMEM((rows, -(-nbrs // left_over), atoms, LANES), f32),
            pltpu.VMEM((2 * OFF, -(-nbrs // left_over), atoms, LANES), f32),
            pltpu.VMEM((RELAYED, OFF, LANES // atoms // 2, atoms, width // LANES * LANES), f32),
            pltpu.VMEM((orb, atoms * atom_count, orb), f32),
            pltpu.VMEM((tiles, orb * orb, 8, LANES), f32),
            pltpu.VMEM((tiles, orb * orb, 8, LANES), f32),
            pltpu.VMEM((rows * width, LANES), f32),
            pltpu.VMEM((orb * orb, 8, LANES), f32),
            pltpu.VMEM((rows * width, LANES), f32),
            pltpu.SemaphoreType.DMA((6,)),
            pltpu.SemaphoreType.DMA((2, piece_count + tiles)),
            pltpu.SemaphoreType.DMA((2, piece_count + tiles)),
            pltpu.SemaphoreType.DMA((RELAYED,)),
            pltpu.SemaphoreType.DMA((RELAYED,)),
            pltpu.SemaphoreType.DMA((max(atom_count - 1, 1),)),
            pltpu.SemaphoreType.DMA((max(atom_count - 1, 1),)),
        ],
        compiler_params=pltpu.CompilerParams(
            collective_id=0, has_side_effects=True, vmem_limit_bytes=48 * 1024 * 1024
        ),
    )(
        *(
            pltpu.with_memory_space_constraint(operand, pltpu.HBM)
            for operand in (
                jnp.transpose(green_blocks, (0, 2, 1, 3)),
                jnp.transpose(coupling, (1, 0, 2)),
                neighbours,
                freq_offset.reshape(1, -1),
                emit_weight.reshape(1, -1),
                absorb_weight.reshape(1, -1),
            )
        )
    )
    return jnp.transpose(result, (0, 2, 1, 3))


def solution(mesh):
    placed = (
        P("energy", "atom", None, None),
        P("atom", None, None),
        P("atom", None),
        P(),
        P(),
        P(),
    )
    return jax.shard_map(
        functools.partial(local, mesh.shape["energy"], mesh.shape["atom"]),
        mesh=mesh,
        in_specs=placed,
        out_specs=P("energy", "atom", None, None),
        check_vma=False,
    )
```

```python
import functools

import jax
import jax.numpy as jnp
from jax import lax
from jax.experimental import pallas as pl
from jax.experimental.pallas import tpu as pltpu
from jax.sharding import PartitionSpec as P

OFF = 2
RELAYED = 3
LANES = 128
MESH = pl.DeviceIdType.MESH


def kernel(
    energy_count,
    atom_count,
    x_ref,
    coup_hbm,
    nbr_hbm,
    freq_hbm,
    emit_hbm,
    absorb_hbm,
    out_ref,
    coup_ref,
    nbr_ref,
    freq_ref,
    emit_ref,
    absorb_ref,
    gbuf,
    packed,
    arrived,
    relay,
    call,
    right_coef,
    left_coef,
    xt,
    mid,
    ot,
    load_sem,
    halo_send,
    halo_recv,
    relay_send,
    relay_recv,
    coup_send,
    coup_recv,
):
    rows, nbrs, atoms, width = x_ref.shape
    orb = coup_hbm.shape[0]
    cells = orb * orb
    per_tile = LANES // atoms
    tiles = -(-nbrs // per_tile)
    spans = [(t * per_tile, min(per_tile, nbrs - t * per_tile)) for t in range(tiles)]
    full = width // LANES * LANES
    rest = width - full
    groups = LANES // rest
    packs = [(t * per_tile // groups, -(-(spans[t][0] + spans[t][1]) // groups) - t * per_tile // groups) for t in range(tiles)]
    raw = [t for t in range(tiles) if t == 0 or spans[t][1] < per_tile]
    owned = [t for t in range(tiles) if t not in raw]
    all_atoms = atoms * atom_count
    half = per_tile // 2
    pieces = [(start, min(half, nbrs - start)) for start in range(0, nbrs, half)]
    held_by = {t: [p for p, (start, _) in enumerate(pieces) if start // per_tile == t] for t in range(tiles)}

    me_e = lax.axis_index("energy")
    me_a = lax.axis_index("atom")
    has_left = me_e > 0
    has_right = me_e < energy_count - 1

    barrier = pltpu.get_barrier_semaphore()

    def greet(e, a):
        pl.semaphore_signal(barrier, inc=1, device_id=(e, a), device_id_type=MESH)

    @pl.when(has_left)
    def _():
        greet(me_e - 1, me_a)

    @pl.when(has_right)
    def _():
        greet(me_e + 1, me_a)

    @pl.when(me_e > 1)
    def _():
        greet(me_e - 2, me_a)

    @pl.when(me_e < energy_count - 2)
    def _():
        greet(me_e + 2, me_a)

    partners = [lax.rem(me_a + k, atom_count) for k in range(1, atom_count)]
    for partner in partners:
        greet(me_e, partner)
    loads = []
    for k, (src, dst) in enumerate(
        [
            (x_ref, gbuf.at[pl.ds(OFF, rows), pl.ds(0, nbrs)]),
            (coup_hbm, coup_ref),
            (nbr_hbm, nbr_ref),
            (freq_hbm, freq_ref),
            (emit_hbm, emit_ref),
            (absorb_hbm, absorb_ref),
        ]
    ):
        copy = pltpu.make_async_copy(src, dst, load_sem.at[k])
        copy.start()
        loads.append(copy)

    for copy in loads[1:]:
        copy.wait()
    freq = freq_ref[...]

    def weight(ref, step):
        return jnp.sum(jnp.where(freq == step, ref[...], 0.0), axis=1, keepdims=True)

    weights = [
        (0, weight(emit_ref, 2)),
        (1, weight(emit_ref, 1)),
        (3, weight(absorb_ref, 1)),
        (4, weight(absorb_ref, 2)),
    ]

    lanes = tiles * LANES
    slot = lax.broadcasted_iota(jnp.int32, (nbrs, lanes), 0)
    pair = lax.broadcasted_iota(jnp.int32, (nbrs, lanes), 1)
    spread = jnp.where(pair // atoms == slot, 1.0, 0.0).astype(jnp.float32)
    listed = jnp.dot(
        nbr_ref[...].astype(jnp.float32), spread, preferred_element_type=jnp.float32, precision=lax.Precision.HIGHEST
    )
    atom_row = lax.broadcasted_iota(jnp.int32, (atoms, lanes), 0)
    atom_pair = lax.broadcasted_iota(jnp.int32, (atoms, lanes), 1)
    own = jnp.where(atom_pair % atoms == atom_row, 1.0, 0.0).astype(jnp.float32)
    index = jnp.sum(listed * own, axis=0, keepdims=True)
    ids = lax.broadcasted_iota(jnp.int32, (all_atoms, lanes), 0).astype(jnp.float32)
    chosen = jnp.where(ids == index, 1.0, 0.0).astype(jnp.float32)

    outer = jnp.logical_or(me_e == 0, me_e == energy_count - 1)
    beside = jnp.logical_or(me_e == 1, me_e == energy_count - 2)

    @pl.when(outer)
    def _():
        pl.semaphore_wait(barrier, atom_count + 1)

    @pl.when(beside)
    def _():
        pl.semaphore_wait(barrier, atom_count + 2)

    @pl.when(jnp.logical_not(jnp.logical_or(outer, beside)))
    def _():
        pl.semaphore_wait(barrier, atom_count + 3)

    def own_rows(p, row):
        start, count = pieces[p]
        ref, row = (x_ref, row) if start // per_tile in raw else (gbuf, row + OFF)
        return ref.at[pl.ds(row, OFF), pl.ds(start, count), :, pl.ds(0, full)]

    def halo(p, to_right):
        src_row, dst_row, side = (rows - OFF, 0, 0) if to_right else (0, rows + OFF, 1)
        if p >= len(pieces):
            first, count = packs[p - len(pieces)]
            src = packed.at[pl.ds(src_row, OFF), pl.ds(first, count)]
            dst = arrived.at[pl.ds(side * OFF, OFF), pl.ds(first, count)]
        else:
            start, count = pieces[p]
            src = own_rows(p, src_row)
            dst = gbuf.at[pl.ds(dst_row, OFF), pl.ds(start, count), :, pl.ds(0, full)]
        return pltpu.make_async_remote_copy(
            src_ref=src,
            dst_ref=dst,
            send_sem=halo_send.at[side, p],
            recv_sem=halo_recv.at[side, p],
            device_id=(me_e + 1 if to_right else me_e - 1, me_a),
            device_id_type=MESH,
        )

    pairs = energy_count // 2
    mine = lax.div(me_e, 2)
    odd = lax.rem(me_e, 2) == 1
    even = lax.rem(me_e, 2) == 0
    via_right = lax.div((RELAYED + 1) * (pairs - 1 - mine), pairs)
    via_left = lax.div((RELAYED + 1) * mine, pairs)

    def detour(p, to_right):
        src_row, side = (rows - OFF, 0) if to_right else (0, 1)
        return pltpu.make_async_remote_copy(
            src_ref=own_rows(p, src_row),
            dst_ref=relay.at[p],
            send_sem=halo_send.at[side, p],
            recv_sem=relay_recv.at[p],
            device_id=(me_e - 1 if to_right else me_e + 1, me_a),
            device_id_type=MESH,
        )

    def passed_on(p, to_right):
        start, count = pieces[p]
        dst_row, side = (0, 0) if to_right else (rows + OFF, 1)
        return pltpu.make_async_remote_copy(
            src_ref=relay.at[p],
            dst_ref=gbuf.at[pl.ds(dst_row, OFF), pl.ds(start, count), :, pl.ds(0, full)],
            send_sem=relay_send.at[p],
            recv_sem=halo_recv.at[side, p],
            device_id=(me_e + 2 if to_right else me_e - 2, me_a),
            device_id_type=MESH,
        )

    def send(p):
        if p < RELAYED:
            around_right = jnp.logical_and(odd, p < via_right)
            around_left = jnp.logical_and(even, p < via_left)

            @pl.when(around_right)
            def _():
                detour(p, True).start()

            @pl.when(around_left)
            def _():
                detour(p, False).start()

            straight_right = jnp.logical_and(has_right, jnp.logical_not(around_right))
            straight_left = jnp.logical_and(has_left, jnp.logical_not(around_left))
        else:
            straight_right, straight_left = has_right, has_left

        @pl.when(straight_right)
        def _():
            halo(p, True).start()

        @pl.when(straight_left)
        def _():
            halo(p, False).start()

    def forward(p):
        @pl.when(jnp.logical_and(odd, p < via_left))
        def _():
            detour(p, False).wait_recv()
            passed_on(p, False).start()

        @pl.when(jnp.logical_and(even, p < via_right))
        def _():
            detour(p, True).wait_recv()
            passed_on(p, True).start()

    def receive(p):
        @pl.when(has_left)
        def _():
            halo(p, True).wait_recv()

        @pl.when(has_right)
        def _():
            halo(p, False).wait_recv()

    coup_copies = []
    for k, partner in enumerate(partners):
        copy = pltpu.make_async_remote_copy(
            src_ref=coup_hbm,
            dst_ref=call.at[:, pl.ds(pl.multiple_of(me_a * atoms, atoms), atoms)],
            send_sem=coup_send.at[k],
            recv_sem=coup_recv.at[k],
            device_id=(me_e, partner),
            device_id_type=MESH,
        )
        copy.start()
        coup_copies.append(copy)

    for t in raw:
        for p in held_by[t]:
            send(p)

    loads[0].wait()
    gbuf[OFF : OFF + rows, nbrs:] = jnp.zeros((rows, gbuf.shape[1] - nbrs) + gbuf.shape[2:], jnp.float32)

    def send_packed(t):
        first, count = packs[t]

        def pack(m, carry):
            for e in range(rows):
                packed[e, m] = jnp.concatenate(
                    [gbuf[OFF + e, m * groups + k, :, full:] for k in range(groups)], axis=-1
                )
            return carry

        lax.fori_loop(first, first + count, pack, 0)
        send(len(pieces) + t)

    for t in raw:
        send_packed(t)

    call[:, pl.ds(pl.multiple_of(me_a * atoms, atoms), atoms), :] = coup_ref[...]

    @pl.when(jnp.logical_not(has_left))
    def _():
        gbuf[0:OFF] = jnp.zeros((OFF,) + gbuf.shape[1:], jnp.float32)
        arrived[0:OFF] = jnp.zeros((OFF,) + arrived.shape[1:], jnp.float32)

    @pl.when(jnp.logical_not(has_right))
    def _():
        gbuf[rows + OFF : rows + 2 * OFF] = jnp.zeros((OFF,) + gbuf.shape[1:], jnp.float32)
        arrived[OFF : 2 * OFF] = jnp.zeros((OFF,) + arrived.shape[1:], jnp.float32)

    def expand(source, select, target, t):
        def one(a, carry):
            table = lax.dot_general(
                source[a],
                select[:, t * LANES : (t + 1) * LANES],
                (((0,), (0,)), ((), ())),
                preferred_element_type=jnp.float32,
                precision=lax.Precision.HIGHEST,
            )
            for d in range(orb):
                target[t, a * orb + d] = jnp.broadcast_to(table[d : d + 1], (8, LANES))
            return carry

        lax.fori_loop(0, orb, one, 0, unroll=4)

    for t in owned:
        expand(coup_ref, own, left_coef, t)
    for copy in coup_copies:
        copy.wait()
    for t in owned:
        expand(call, chosen, right_coef, t)

    def dress(t, read, write):
        for e in range(rows):
            xt[e * width : (e + 1) * width, :] = jnp.transpose(read(e))

        def times_right(pair, carry):
            first = pair * 2
            held = [
                jnp.stack([xt[pl.ds((first + k) * orb + d, 8, stride=cells), :] for d in range(orb)])
                for k in range(2)
            ]
            for f in range(orb):
                factor = right_coef[t, f * orb : (f + 1) * orb]
                for k in range(2):
                    mid[f * orb + first + k] = jnp.sum(factor * held[k], axis=0)
            return carry

        lax.fori_loop(0, orb // 2, times_right, 0)

        def times_left(pair, carry):
            first = pair * 2
            held = [mid[pl.ds((first + k) * orb, orb)] for k in range(2)]
            for a in range(orb):
                factor = left_coef[t, a * orb : (a + 1) * orb]
                for k in range(2):
                    ot[pl.ds(a * orb + first + k, 8, stride=cells), :] = jnp.sum(factor * held[k], axis=0)
            return carry

        lax.fori_loop(0, orb // 2, times_left, 0)

        for e in range(rows):
            write(e, jnp.transpose(ot[e * width : (e + 1) * width, :]))

    def filtered(e, start, count):
        total = None
        for step, factor in weights:
            term = gbuf[e + step, pl.ds(start, count)].reshape(count * atoms, width) * factor
            total = term if total is None else total + term
        return total

    def receive_packed(t):
        first, count = packs[t]
        receive(len(pieces) + t)

        def unpack(m, carry):
            for row in range(2 * OFF):
                piece = arrived[row, m]
                target = row if row < OFF else rows + row
                for k in range(groups):
                    gbuf[target, m * groups + k, :, full:] = piece[:, k * rest : (k + 1) * rest]
            return carry

        lax.fori_loop(first, first + count, unpack, 0)

    for t in owned:
        start, count = spans[t]

        def write(e, block):
            gbuf[OFF + e, start : start + per_tile] = block.reshape(per_tile, atoms, width)

        dress(t, lambda e: gbuf[OFF + e, start : start + per_tile].reshape(LANES, width), write)
        for p in held_by[t]:
            send(p)
        send_packed(t)

    forward(0)
    for t in raw:
        expand(coup_ref, own, left_coef, t)
        expand(call, chosen, right_coef, t)
    for p in range(1, RELAYED - 1):
        forward(p)

    for place, t in enumerate(raw):
        start, count = spans[t]

        def write(e, block):
            out_ref[e, start : start + count] = block[: count * atoms].reshape(count, atoms, width)

        for p in held_by[t]:
            receive(p)
        receive_packed(t)
        dress(t, lambda e: filtered(e, start, per_tile), write)
        if place == 0:
            forward(RELAYED - 1)

    for t in owned:
        receive_packed(t)
        for p in held_by[t]:
            start, count = pieces[p]
            receive(p)
            for e in range(rows):
                out_ref[e, start : start + count] = filtered(e, start, count).reshape(count, atoms, width)

    for p in range(len(pieces) + tiles):

        @pl.when(has_right)
        def _():
            halo(p, True).wait_send()

        @pl.when(has_left)
        def _():
            halo(p, False).wait_send()

    for p in range(RELAYED):

        @pl.when(jnp.logical_and(odd, p < via_left))
        def _():
            passed_on(p, False).wait_send()

        @pl.when(jnp.logical_and(even, p < via_right))
        def _():
            passed_on(p, True).wait_send()


def local(energy_count, atom_count, green_blocks, coupling, neighbours, freq_offset, emit_weight, absorb_weight):
    rows, atoms, nbrs, width = green_blocks.shape
    orb = coupling.shape[1]
    tiles = -(-(nbrs * atoms) // LANES)
    padded = tiles * LANES // atoms
    hbm = pl.BlockSpec(memory_space=pltpu.HBM)
    piece_count = -(-nbrs // (LANES // atoms // 2))
    left_over = LANES // (width % LANES)
    f32 = jnp.float32
    result = pl.pallas_call(
        functools.partial(kernel, energy_count, atom_count),
        out_shape=pltpu.VMEM((rows, nbrs, atoms, width), f32),
        in_specs=[hbm] * 6,
        out_specs=pl.BlockSpec(memory_space=pltpu.VMEM),
        scratch_shapes=[
            pltpu.VMEM((orb, atoms, orb), f32),
            pltpu.VMEM((atoms, nbrs), jnp.int32),
            pltpu.VMEM((1, freq_offset.shape[0]), jnp.int32),
            pltpu.VMEM((1, freq_offset.shape[0]), f32),
            pltpu.VMEM((1, freq_offset.shape[0]), f32),
            pltpu.VMEM((rows + 2 * OFF, padded, atoms, width), f32),
            pltpu.VMEM((rows, -(-nbrs // left_over), atoms, LANES), f32),
            pltpu.VMEM((2 * OFF, -(-nbrs // left_over), atoms, LANES), f32),
            pltpu.VMEM((RELAYED, OFF, LANES // atoms // 2, atoms, width // LANES * LANES), f32),
            pltpu.VMEM((orb, atoms * atom_count, orb), f32),
            pltpu.VMEM((tiles, orb * orb, 8, LANES), f32),
            pltpu.VMEM((tiles, orb * orb, 8, LANES), f32),
            pltpu.VMEM((rows * width, LANES), f32),
            pltpu.VMEM((orb * orb, 8, LANES), f32),
            pltpu.VMEM((rows * width, LANES), f32),
            pltpu.SemaphoreType.DMA((6,)),
            pltpu.SemaphoreType.DMA((2, piece_count + tiles)),
            pltpu.SemaphoreType.DMA((2, piece_count + tiles)),
            pltpu.SemaphoreType.DMA((RELAYED,)),
            pltpu.SemaphoreType.DMA((RELAYED,)),
            pltpu.SemaphoreType.DMA((max(atom_count - 1, 1),)),
            pltpu.SemaphoreType.DMA((max(atom_count - 1, 1),)),
        ],
        compiler_params=pltpu.CompilerParams(
            collective_id=0, has_side_effects=True, vmem_limit_bytes=48 * 1024 * 1024
        ),
    )(
        *(
            pltpu.with_memory_space_constraint(operand, pltpu.HBM)
            for operand in (
                jnp.transpose(green_blocks, (0, 2, 1, 3)),
                jnp.transpose(coupling, (1, 0, 2)),
                neighbours,
                freq_offset.reshape(1, -1),
                emit_weight.reshape(1, -1),
                absorb_weight.reshape(1, -1),
            )
        )
    )
    return jnp.transpose(result, (0, 2, 1, 3))


def solution(mesh):
    placed = (
        P("energy", "atom", None, None),
        P("atom", None, None),
        P("atom", None),
        P(),
        P(),
        P(),
    )
    return jax.shard_map(
        functools.partial(local, mesh.shape["energy"], mesh.shape["atom"]),
        mesh=mesh,
        in_specs=placed,
        out_specs=P("energy", "atom", None, None),
        check_vma=False,
    )
```

```python
import functools

import jax
import jax.numpy as jnp
from jax import lax
from jax.experimental import pallas as pl
from jax.experimental.pallas import tpu as pltpu
from jax.sharding import PartitionSpec as P

OFF = 2
RELAYED = 3
LANES = 128
MESH = pl.DeviceIdType.MESH


def kernel(
    energy_count,
    atom_count,
    x_ref,
    coup_hbm,
    nbr_hbm,
    freq_hbm,
    emit_hbm,
    absorb_hbm,
    out_ref,
    coup_ref,
    nbr_ref,
    freq_ref,
    emit_ref,
    absorb_ref,
    gmain,
    grest,
    packed,
    arrived,
    relay,
    call,
    right_coef,
    left_coef,
    xt,
    mid,
    ot,
    load_sem,
    halo_send,
    halo_recv,
    relay_send,
    relay_recv,
    coup_send,
    coup_recv,
):
    rows, nbrs, atoms, width = x_ref.shape
    orb = coup_hbm.shape[0]
    cells = orb * orb
    per_tile = LANES // atoms
    tiles = -(-nbrs // per_tile)
    spans = [(t * per_tile, min(per_tile, nbrs - t * per_tile)) for t in range(tiles)]
    full = width // LANES * LANES
    rest = width - full
    groups = LANES // rest
    packs = [(t * per_tile // groups, -(-(spans[t][0] + spans[t][1]) // groups) - t * per_tile // groups) for t in range(tiles)]
    raw = [t for t in range(tiles) if t == 0 or spans[t][1] < per_tile]
    owned = [t for t in range(tiles) if t not in raw]
    all_atoms = atoms * atom_count
    half = per_tile // 2
    pieces = [(start, min(half, nbrs - start)) for start in range(0, nbrs, half)]
    held_by = {t: [p for p, (start, _) in enumerate(pieces) if start // per_tile == t] for t in range(tiles)}

    me_e = lax.axis_index("energy")
    me_a = lax.axis_index("atom")
    has_left = me_e > 0
    has_right = me_e < energy_count - 1

    barrier = pltpu.get_barrier_semaphore()

    def greet(e, a):
        pl.semaphore_signal(barrier, inc=1, device_id=(e, a), device_id_type=MESH)

    @pl.when(has_left)
    def _():
        greet(me_e - 1, me_a)

    @pl.when(has_right)
    def _():
        greet(me_e + 1, me_a)

    @pl.when(me_e > 1)
    def _():
        greet(me_e - 2, me_a)

    @pl.when(me_e < energy_count - 2)
    def _():
        greet(me_e + 2, me_a)

    partners = [lax.rem(me_a + k, atom_count) for k in range(1, atom_count)]
    for partner in partners:
        greet(me_e, partner)
    loads = []
    for k, (src, dst) in enumerate(
        [
            (x_ref.at[:, :, :, pl.ds(0, full)], gmain.at[pl.ds(OFF, rows), pl.ds(0, nbrs)]),
            (x_ref.at[:, :, :, pl.ds(full, rest)], grest.at[pl.ds(OFF, rows), pl.ds(0, nbrs)]),
            (coup_hbm, coup_ref),
            (nbr_hbm, nbr_ref),
            (freq_hbm, freq_ref),
            (emit_hbm, emit_ref),
            (absorb_hbm, absorb_ref),
        ]
    ):
        copy = pltpu.make_async_copy(src, dst, load_sem.at[k])
        copy.start()
        loads.append(copy)

    for copy in loads[2:]:
        copy.wait()
    freq = freq_ref[...]

    def weight(ref, step):
        return jnp.sum(jnp.where(freq == step, ref[...], 0.0), axis=1, keepdims=True)

    weights = [
        (0, weight(emit_ref, 2)),
        (1, weight(emit_ref, 1)),
        (3, weight(absorb_ref, 1)),
        (4, weight(absorb_ref, 2)),
    ]

    lanes = tiles * LANES
    slot = lax.broadcasted_iota(jnp.int32, (nbrs, lanes), 0)
    pair = lax.broadcasted_iota(jnp.int32, (nbrs, lanes), 1)
    spread = jnp.where(pair // atoms == slot, 1.0, 0.0).astype(jnp.float32)
    listed = jnp.dot(
        nbr_ref[...].astype(jnp.float32), spread, preferred_element_type=jnp.float32, precision=lax.Precision.HIGHEST
    )
    atom_row = lax.broadcasted_iota(jnp.int32, (atoms, lanes), 0)
    atom_pair = lax.broadcasted_iota(jnp.int32, (atoms, lanes), 1)
    own = jnp.where(atom_pair % atoms == atom_row, 1.0, 0.0).astype(jnp.float32)
    index = jnp.sum(listed * own, axis=0, keepdims=True)
    ids = lax.broadcasted_iota(jnp.int32, (all_atoms, lanes), 0).astype(jnp.float32)
    chosen = jnp.where(ids == index, 1.0, 0.0).astype(jnp.float32)

    outer = jnp.logical_or(me_e == 0, me_e == energy_count - 1)
    beside = jnp.logical_or(me_e == 1, me_e == energy_count - 2)

    @pl.when(outer)
    def _():
        pl.semaphore_wait(barrier, atom_count + 1)

    @pl.when(beside)
    def _():
        pl.semaphore_wait(barrier, atom_count + 2)

    @pl.when(jnp.logical_not(jnp.logical_or(outer, beside)))
    def _():
        pl.semaphore_wait(barrier, atom_count + 3)

    def own_rows(p, row):
        start, count = pieces[p]
        return gmain.at[pl.ds(row + OFF, OFF), pl.ds(start, count)]

    def halo(p, to_right):
        src_row, dst_row, side = (rows - OFF, 0, 0) if to_right else (0, rows + OFF, 1)
        if p >= len(pieces):
            first, count = packs[p - len(pieces)]
            src = packed.at[pl.ds(src_row, OFF), pl.ds(first, count)]
            dst = arrived.at[pl.ds(side * OFF, OFF), pl.ds(first, count)]
        else:
            start, count = pieces[p]
            src = own_rows(p, src_row)
            dst = gmain.at[pl.ds(dst_row, OFF), pl.ds(start, count)]
        return pltpu.make_async_remote_copy(
            src_ref=src,
            dst_ref=dst,
            send_sem=halo_send.at[side, p],
            recv_sem=halo_recv.at[side, p],
            device_id=(me_e + 1 if to_right else me_e - 1, me_a),
            device_id_type=MESH,
        )

    pairs = energy_count // 2
    mine = lax.div(me_e, 2)
    odd = lax.rem(me_e, 2) == 1
    even = lax.rem(me_e, 2) == 0
    via_right = lax.div((RELAYED + 1) * (pairs - 1 - mine), pairs)
    via_left = lax.div((RELAYED + 1) * mine, pairs)

    def detour(p, to_right):
        src_row, side = (rows - OFF, 0) if to_right else (0, 1)
        return pltpu.make_async_remote_copy(
            src_ref=own_rows(p, src_row),
            dst_ref=relay.at[p],
            send_sem=halo_send.at[side, p],
            recv_sem=relay_recv.at[p],
            device_id=(me_e - 1 if to_right else me_e + 1, me_a),
            device_id_type=MESH,
        )

    def passed_on(p, to_right):
        start, count = pieces[p]
        dst_row, side = (0, 0) if to_right else (rows + OFF, 1)
        return pltpu.make_async_remote_copy(
            src_ref=relay.at[p],
            dst_ref=gmain.at[pl.ds(dst_row, OFF), pl.ds(start, count)],
            send_sem=relay_send.at[p],
            recv_sem=halo_recv.at[side, p],
            device_id=(me_e + 2 if to_right else me_e - 2, me_a),
            device_id_type=MESH,
        )

    def send(p):
        if p < RELAYED:
            around_right = jnp.logical_and(odd, p < via_right)
            around_left = jnp.logical_and(even, p < via_left)

            @pl.when(around_right)
            def _():
                detour(p, True).start()

            @pl.when(around_left)
            def _():
                detour(p, False).start()

            straight_right = jnp.logical_and(has_right, jnp.logical_not(around_right))
            straight_left = jnp.logical_and(has_left, jnp.logical_not(around_left))
        else:
            straight_right, straight_left = has_right, has_left

        @pl.when(straight_right)
        def _():
            halo(p, True).start()

        @pl.when(straight_left)
        def _():
            halo(p, False).start()

    def forward(p):
        @pl.when(jnp.logical_and(odd, p < via_left))
        def _():
            detour(p, False).wait_recv()
            passed_on(p, False).start()

        @pl.when(jnp.logical_and(even, p < via_right))
        def _():
            detour(p, True).wait_recv()
            passed_on(p, True).start()

    def receive(p):
        @pl.when(has_left)
        def _():
            halo(p, True).wait_recv()

        @pl.when(has_right)
        def _():
            halo(p, False).wait_recv()

    coup_copies = []
    for k, partner in enumerate(partners):
        copy = pltpu.make_async_remote_copy(
            src_ref=coup_hbm,
            dst_ref=call.at[:, pl.ds(pl.multiple_of(me_a * atoms, atoms), atoms)],
            send_sem=coup_send.at[k],
            recv_sem=coup_recv.at[k],
            device_id=(me_e, partner),
            device_id_type=MESH,
        )
        copy.start()
        coup_copies.append(copy)

    loads[0].wait()
    for t in raw:
        for p in held_by[t]:
            send(p)

    loads[1].wait()
    for ref in (gmain, grest):
        ref[OFF : OFF + rows, nbrs:] = jnp.zeros((rows, ref.shape[1] - nbrs) + ref.shape[2:], jnp.float32)

    def send_packed(t):
        first, count = packs[t]

        def pack(m, carry):
            for e in range(rows):
                packed[e, m] = jnp.concatenate(
                    [grest[OFF + e, m * groups + k] for k in range(groups)], axis=-1
                )
            return carry

        lax.fori_loop(first, first + count, pack, 0)
        send(len(pieces) + t)

    for t in raw:
        send_packed(t)

    call[:, pl.ds(pl.multiple_of(me_a * atoms, atoms), atoms), :] = coup_ref[...]

    @pl.when(jnp.logical_not(has_left))
    def _():
        for ref in (gmain, grest, arrived):
            ref[0:OFF] = jnp.zeros((OFF,) + ref.shape[1:], jnp.float32)

    @pl.when(jnp.logical_not(has_right))
    def _():
        for ref in (gmain, grest):
            ref[rows + OFF : rows + 2 * OFF] = jnp.zeros((OFF,) + ref.shape[1:], jnp.float32)
        arrived[OFF : 2 * OFF] = jnp.zeros((OFF,) + arrived.shape[1:], jnp.float32)

    def expand(source, select, target, t):
        def one(a, carry):
            table = lax.dot_general(
                source[a],
                select[:, t * LANES : (t + 1) * LANES],
                (((0,), (0,)), ((), ())),
                preferred_element_type=jnp.float32,
                precision=lax.Precision.HIGHEST,
            )
            for d in range(orb):
                target[t, a * orb + d] = jnp.broadcast_to(table[d : d + 1], (8, LANES))
            return carry

        lax.fori_loop(0, orb, one, 0, unroll=4)

    for t in owned:
        expand(coup_ref, own, left_coef, t)
    for copy in coup_copies:
        copy.wait()
    for t in owned:
        expand(call, chosen, right_coef, t)

    def dress(t, read, write):
        for e in range(rows):
            for base, block in zip((0, full), read(e)):
                xt[e * width + base : e * width + base + block.shape[1], :] = jnp.transpose(block)

        def times_right(pair, carry):
            first = pair * 2
            held = [
                jnp.stack([xt[pl.ds((first + k) * orb + d, 8, stride=cells), :] for d in range(orb)])
                for k in range(2)
            ]
            for f in range(orb):
                factor = right_coef[t, f * orb : (f + 1) * orb]
                for k in range(2):
                    mid[f * orb + first + k] = jnp.sum(factor * held[k], axis=0)
            return carry

        lax.fori_loop(0, orb // 2, times_right, 0)

        def times_left(pair, carry):
            first = pair * 2
            held = [mid[pl.ds((first + k) * orb, orb)] for k in range(2)]
            for a in range(orb):
                factor = left_coef[t, a * orb : (a + 1) * orb]
                for k in range(2):
                    ot[pl.ds(a * orb + first + k, 8, stride=cells), :] = jnp.sum(factor * held[k], axis=0)
            return carry

        lax.fori_loop(0, orb // 2, times_left, 0)

        for e in range(rows):
            write(
                e,
                [
                    jnp.transpose(ot[e * width : e * width + full, :]),
                    jnp.transpose(ot[e * width + full : (e + 1) * width, :]),
                ],
            )

    def rows_of(row, start, count):
        return [ref[row, pl.ds(start, count)].reshape(count * atoms, ref.shape[3]) for ref in (gmain, grest)]

    def filtered(e, start, count):
        totals = None
        for step, factor in weights:
            terms = [part * factor for part in rows_of(e + step, start, count)]
            totals = terms if totals is None else [total + term for total, term in zip(totals, terms)]
        return totals

    def write_out(e, start, count, blocks):
        for base, block in zip((0, full), blocks):
            size = block.shape[1]
            out_ref[e, start : start + count, :, base : base + size] = block[: count * atoms].reshape(
                count, atoms, size
            )

    def receive_packed(t):
        first, count = packs[t]
        receive(len(pieces) + t)

        def unpack(m, carry):
            for row in range(2 * OFF):
                piece = arrived[row, m]
                target = row if row < OFF else rows + row
                for k in range(groups):
                    grest[target, m * groups + k] = piece[:, k * rest : (k + 1) * rest]
            return carry

        lax.fori_loop(first, first + count, unpack, 0)

    for t in owned:
        start, count = spans[t]

        def write(e, blocks):
            for ref, block in zip((gmain, grest), blocks):
                ref[OFF + e, start : start + per_tile] = block.reshape(per_tile, atoms, block.shape[1])

        dress(t, lambda e: rows_of(OFF + e, start, per_tile), write)
        for p in held_by[t]:
            send(p)
        send_packed(t)

    forward(0)
    for t in raw:
        expand(coup_ref, own, left_coef, t)
        expand(call, chosen, right_coef, t)
    for p in range(1, RELAYED - 1):
        forward(p)

    for place, t in enumerate(raw):
        start, count = spans[t]

        for p in held_by[t]:
            receive(p)
        receive_packed(t)
        dress(t, lambda e: filtered(e, start, per_tile), lambda e, blocks: write_out(e, start, count, blocks))
        if place == 0:
            forward(RELAYED - 1)

    for t in owned:
        receive_packed(t)
        for p in held_by[t]:
            start, count = pieces[p]
            receive(p)
            for e in range(rows):
                write_out(e, start, count, filtered(e, start, count))

    for p in range(len(pieces) + tiles):

        @pl.when(has_right)
        def _():
            halo(p, True).wait_send()

        @pl.when(has_left)
        def _():
            halo(p, False).wait_send()

    for p in range(RELAYED):

        @pl.when(jnp.logical_and(odd, p < via_left))
        def _():
            passed_on(p, False).wait_send()

        @pl.when(jnp.logical_and(even, p < via_right))
        def _():
            passed_on(p, True).wait_send()


def local(energy_count, atom_count, green_blocks, coupling, neighbours, freq_offset, emit_weight, absorb_weight):
    rows, atoms, nbrs, width = green_blocks.shape
    orb = coupling.shape[1]
    tiles = -(-(nbrs * atoms) // LANES)
    padded = tiles * LANES // atoms
    hbm = pl.BlockSpec(memory_space=pltpu.HBM)
    piece_count = -(-nbrs // (LANES // atoms // 2))
    left_over = LANES // (width % LANES)
    f32 = jnp.float32
    result = pl.pallas_call(
        functools.partial(kernel, energy_count, atom_count),
        out_shape=pltpu.VMEM((rows, nbrs, atoms, width), f32),
        in_specs=[hbm] * 6,
        out_specs=pl.BlockSpec(memory_space=pltpu.VMEM),
        scratch_shapes=[
            pltpu.VMEM((orb, atoms, orb), f32),
            pltpu.VMEM((atoms, nbrs), jnp.int32),
            pltpu.VMEM((1, freq_offset.shape[0]), jnp.int32),
            pltpu.VMEM((1, freq_offset.shape[0]), f32),
            pltpu.VMEM((1, freq_offset.shape[0]), f32),
            pltpu.VMEM((rows + 2 * OFF, padded, atoms, width // LANES * LANES), f32),
            pltpu.VMEM((rows + 2 * OFF, padded, atoms, width % LANES), f32),
            pltpu.VMEM((rows, -(-nbrs // left_over), atoms, LANES), f32),
            pltpu.VMEM((2 * OFF, -(-nbrs // left_over), atoms, LANES), f32),
            pltpu.VMEM((RELAYED, OFF, LANES // atoms // 2, atoms, width // LANES * LANES), f32),
            pltpu.VMEM((orb, atoms * atom_count, orb), f32),
            pltpu.VMEM((tiles, orb * orb, 8, LANES), f32),
            pltpu.VMEM((tiles, orb * orb, 8, LANES), f32),
            pltpu.VMEM((rows * width, LANES), f32),
            pltpu.VMEM((orb * orb, 8, LANES), f32),
            pltpu.VMEM((rows * width, LANES), f32),
            pltpu.SemaphoreType.DMA((7,)),
            pltpu.SemaphoreType.DMA((2, piece_count + tiles)),
            pltpu.SemaphoreType.DMA((2, piece_count + tiles)),
            pltpu.SemaphoreType.DMA((RELAYED,)),
            pltpu.SemaphoreType.DMA((RELAYED,)),
            pltpu.SemaphoreType.DMA((max(atom_count - 1, 1),)),
            pltpu.SemaphoreType.DMA((max(atom_count - 1, 1),)),
        ],
        compiler_params=pltpu.CompilerParams(
            collective_id=0, has_side_effects=True, vmem_limit_bytes=48 * 1024 * 1024
        ),
    )(
        *(
            pltpu.with_memory_space_constraint(operand, pltpu.HBM)
            for operand in (
                jnp.transpose(green_blocks, (0, 2, 1, 3)),
                jnp.transpose(coupling, (1, 0, 2)),
                neighbours,
                freq_offset.reshape(1, -1),
                emit_weight.reshape(1, -1),
                absorb_weight.reshape(1, -1),
            )
        )
    )
    return jnp.transpose(result, (0, 2, 1, 3))


def solution(mesh):
    placed = (
        P("energy", "atom", None, None),
        P("atom", None, None),
        P("atom", None),
        P(),
        P(),
        P(),
    )
    return jax.shard_map(
        functools.partial(local, mesh.shape["energy"], mesh.shape["atom"]),
        mesh=mesh,
        in_specs=placed,
        out_specs=P("energy", "atom", None, None),
        check_vma=False,
    )
```

```python
import functools

import jax
import jax.numpy as jnp
from jax import lax
from jax.experimental import pallas as pl
from jax.experimental.pallas import tpu as pltpu
from jax.sharding import PartitionSpec as P

OFF = 2
QUARTERS = 4
LANES = 128
MESH = pl.DeviceIdType.MESH


def tile_spans(nbrs, per_tile, groups):
    second = (nbrs - per_tile) // 2 // groups * groups
    spans = [(0, per_tile), (per_tile, second), (per_tile + second, nbrs - per_tile - second)]
    assert 0 < second and spans[2][1] <= per_tile
    return spans


def kernel(
    energy_count,
    atom_count,
    x_ref,
    coup_hbm,
    nbr_hbm,
    freq_hbm,
    emit_hbm,
    absorb_hbm,
    out_ref,
    coup_ref,
    nbr_ref,
    freq_ref,
    emit_ref,
    absorb_ref,
    gbuf,
    packed,
    arrived,
    relay,
    relay_packed,
    call,
    right_coef,
    left_coef,
    xt,
    mid,
    ot,
    load_sem,
    halo_send,
    halo_recv,
    relay_send,
    relay_recv,
    coup_send,
    coup_recv,
):
    rows, nbrs, atoms, width = x_ref.shape
    orb = coup_hbm.shape[0]
    cells = orb * orb
    per_tile = LANES // atoms
    spans = tile_spans(nbrs, per_tile, LANES // (width % LANES))
    tiles = len(spans)
    full = width // LANES * LANES
    rest = width - full
    groups = LANES // rest
    packs = [(start // groups, -(-(start + count) // groups) - start // groups) for start, count in spans]
    early = (spans[0][1] + 2) // 2
    pieces = [(0, early), (early, spans[0][1] - early)] + spans[1:]
    held_by = {t: [p for p, (start, _) in enumerate(pieces) if spans[t][0] <= start < sum(spans[t])] for t in range(tiles)}
    level = {0: 1, 2: 2, len(pieces) + 1: 2, 1: 3, len(pieces): 3}
    raw = list(range(tiles - 1))[::-1]
    owned = [tiles - 1]
    all_atoms = atoms * atom_count

    me_e = lax.axis_index("energy")
    me_a = lax.axis_index("atom")
    has_left = me_e > 0
    has_right = me_e < energy_count - 1

    barrier = pltpu.get_barrier_semaphore()

    def greet(e, a):
        pl.semaphore_signal(barrier, inc=1, device_id=(e, a), device_id_type=MESH)

    @pl.when(has_left)
    def _():
        greet(me_e - 1, me_a)

    @pl.when(has_right)
    def _():
        greet(me_e + 1, me_a)

    @pl.when(me_e > 1)
    def _():
        greet(me_e - 2, me_a)

    @pl.when(me_e < energy_count - 2)
    def _():
        greet(me_e + 2, me_a)

    partners = [lax.rem(me_a + k, atom_count) for k in range(1, atom_count)]
    for partner in partners:
        greet(me_e, partner)
    loads = []
    for k, (src, dst) in enumerate(
        [
            (x_ref, gbuf.at[pl.ds(OFF, rows), pl.ds(0, nbrs)]),
            (coup_hbm, coup_ref),
            (nbr_hbm, nbr_ref),
            (freq_hbm, freq_ref),
            (emit_hbm, emit_ref),
            (absorb_hbm, absorb_ref),
        ]
    ):
        copy = pltpu.make_async_copy(src, dst, load_sem.at[k])
        copy.start()
        loads.append(copy)

    for copy in loads[1:]:
        copy.wait()
    freq = freq_ref[...]

    def weight(ref, step):
        return jnp.sum(jnp.where(freq == step, ref[...], 0.0), axis=1, keepdims=True)

    weights = [
        (0, weight(emit_ref, 2)),
        (1, weight(emit_ref, 1)),
        (3, weight(absorb_ref, 1)),
        (4, weight(absorb_ref, 2)),
    ]

    lanes = tiles * LANES
    slot = lax.broadcasted_iota(jnp.int32, (nbrs, lanes), 0)
    pair = lax.broadcasted_iota(jnp.int32, (nbrs, lanes), 1)
    listed_slot = pair // atoms
    for t in range(1, tiles):
        move = spans[t][0] - t * per_tile
        listed_slot = jnp.where(pair // LANES == t, pair // atoms + move, listed_slot)
    spread = jnp.where(listed_slot == slot, 1.0, 0.0).astype(jnp.float32)
    listed = jnp.dot(
        nbr_ref[...].astype(jnp.float32), spread, preferred_element_type=jnp.float32, precision=lax.Precision.HIGHEST
    )
    atom_row = lax.broadcasted_iota(jnp.int32, (atoms, lanes), 0)
    atom_pair = lax.broadcasted_iota(jnp.int32, (atoms, lanes), 1)
    own = jnp.where(atom_pair % atoms == atom_row, 1.0, 0.0).astype(jnp.float32)
    index = jnp.sum(listed * own, axis=0, keepdims=True)
    ids = lax.broadcasted_iota(jnp.int32, (all_atoms, lanes), 0).astype(jnp.float32)
    chosen = jnp.where(ids == index, 1.0, 0.0).astype(jnp.float32)

    outer = jnp.logical_or(me_e == 0, me_e == energy_count - 1)
    beside = jnp.logical_or(me_e == 1, me_e == energy_count - 2)

    @pl.when(outer)
    def _():
        pl.semaphore_wait(barrier, atom_count + 1)

    @pl.when(beside)
    def _():
        pl.semaphore_wait(barrier, atom_count + 2)

    @pl.when(jnp.logical_not(jnp.logical_or(outer, beside)))
    def _():
        pl.semaphore_wait(barrier, atom_count + 3)

    def own_rows(p, row):
        start, count = pieces[p]
        ref, row = (x_ref, row) if start < spans[-1][0] else (gbuf, row + OFF)
        return ref.at[pl.ds(row, OFF), pl.ds(start, count), :, pl.ds(0, full)]

    def halo(p, to_right):
        src_row, dst_row, side = (rows - OFF, 0, 0) if to_right else (0, rows + OFF, 1)
        if p >= len(pieces):
            first, count = packs[p - len(pieces)]
            src = packed.at[pl.ds(src_row, OFF), pl.ds(first, count)]
            dst = arrived.at[pl.ds(side * OFF, OFF), pl.ds(first, count)]
        else:
            start, count = pieces[p]
            src = own_rows(p, src_row)
            dst = gbuf.at[pl.ds(dst_row, OFF), pl.ds(start, count), :, pl.ds(0, full)]
        return pltpu.make_async_remote_copy(
            src_ref=src,
            dst_ref=dst,
            send_sem=halo_send.at[side, p],
            recv_sem=halo_recv.at[side, p],
            device_id=(me_e + 1 if to_right else me_e - 1, me_a),
            device_id_type=MESH,
        )

    pairs = energy_count // 2
    mine = lax.div(me_e, 2)
    odd = lax.rem(me_e, 2) == 1
    even = lax.rem(me_e, 2) == 0
    via_right = lax.div(QUARTERS * (pairs - 1 - mine), pairs)
    via_left = lax.div(QUARTERS * mine, pairs)

    def ends_of(p, to_right):
        src_row, dst_row, side = (rows - OFF, 0, 0) if to_right else (0, rows + OFF, 1)
        if p >= len(pieces):
            first, count = packs[p - len(pieces)]
            src = packed.at[pl.ds(src_row, OFF), pl.ds(first, count)]
            dst = arrived.at[pl.ds(side * OFF, OFF), pl.ds(first, count)]
            return src, relay_packed.at[:, pl.ds(first, count)], dst, side
        start, count = pieces[p]
        dst = gbuf.at[pl.ds(dst_row, OFF), pl.ds(start, count), :, pl.ds(0, full)]
        return own_rows(p, src_row), relay.at[:, pl.ds(start, count)], dst, side

    def detour(p, to_right):
        src, middle, _, side = ends_of(p, to_right)
        return pltpu.make_async_remote_copy(
            src_ref=src,
            dst_ref=middle,
            send_sem=halo_send.at[side, p],
            recv_sem=relay_recv.at[p],
            device_id=(me_e - 1 if to_right else me_e + 1, me_a),
            device_id_type=MESH,
        )

    def passed_on(p, to_right):
        _, middle, dst, side = ends_of(p, to_right)
        return pltpu.make_async_remote_copy(
            src_ref=middle,
            dst_ref=dst,
            send_sem=relay_send.at[p],
            recv_sem=halo_recv.at[side, p],
            device_id=(me_e + 2 if to_right else me_e - 2, me_a),
            device_id_type=MESH,
        )

    def send(p):
        if p in level:
            around_right = jnp.logical_and(odd, via_right >= level[p])
            around_left = jnp.logical_and(even, via_left >= level[p])

            @pl.when(around_right)
            def _():
                detour(p, True).start()

            @pl.when(around_left)
            def _():
                detour(p, False).start()

            straight_right = jnp.logical_and(has_right, jnp.logical_not(around_right))
            straight_left = jnp.logical_and(has_left, jnp.logical_not(around_left))
        else:
            straight_right, straight_left = has_right, has_left

        @pl.when(straight_right)
        def _():
            halo(p, True).start()

        @pl.when(straight_left)
        def _():
            halo(p, False).start()

    def forward(p):
        @pl.when(jnp.logical_and(odd, via_left >= level[p]))
        def _():
            detour(p, False).wait_recv()
            passed_on(p, False).start()

        @pl.when(jnp.logical_and(even, via_right >= level[p]))
        def _():
            detour(p, True).wait_recv()
            passed_on(p, True).start()

    def receive(p):
        @pl.when(has_left)
        def _():
            halo(p, True).wait_recv()

        @pl.when(has_right)
        def _():
            halo(p, False).wait_recv()

    coup_copies = []
    for k, partner in enumerate(partners):
        copy = pltpu.make_async_remote_copy(
            src_ref=coup_hbm,
            dst_ref=call.at[:, pl.ds(pl.multiple_of(me_a * atoms, atoms), atoms)],
            send_sem=coup_send.at[k],
            recv_sem=coup_recv.at[k],
            device_id=(me_e, partner),
            device_id_type=MESH,
        )
        copy.start()
        coup_copies.append(copy)

    for p in sorted((p for p in level if p < len(pieces)), key=level.get):
        send(p)

    loads[0].wait()
    gbuf[OFF : OFF + rows, nbrs:] = jnp.zeros((rows, gbuf.shape[1] - nbrs) + gbuf.shape[2:], jnp.float32)

    def send_packed(t):
        first, count = packs[t]

        def pack(m, carry):
            for e in range(rows):
                packed[e, m] = jnp.concatenate(
                    [gbuf[OFF + e, m * groups + k, :, full:] for k in range(groups)], axis=-1
                )
            return carry

        lax.fori_loop(first, first + count, pack, 0)
        send(len(pieces) + t)

    for t in raw:
        send_packed(t)

    call[:, pl.ds(pl.multiple_of(me_a * atoms, atoms), atoms), :] = coup_ref[...]

    @pl.when(jnp.logical_not(has_left))
    def _():
        gbuf[0:OFF] = jnp.zeros((OFF,) + gbuf.shape[1:], jnp.float32)
        arrived[0:OFF] = jnp.zeros((OFF,) + arrived.shape[1:], jnp.float32)

    @pl.when(jnp.logical_not(has_right))
    def _():
        gbuf[rows + OFF : rows + 2 * OFF] = jnp.zeros((OFF,) + gbuf.shape[1:], jnp.float32)
        arrived[OFF : 2 * OFF] = jnp.zeros((OFF,) + arrived.shape[1:], jnp.float32)

    def expand(source, select, target, t):
        def one(a, carry):
            table = lax.dot_general(
                source[a],
                select[:, t * LANES : (t + 1) * LANES],
                (((0,), (0,)), ((), ())),
                preferred_element_type=jnp.float32,
                precision=lax.Precision.HIGHEST,
            )
            for d in range(orb):
                target[t, a * orb + d] = jnp.broadcast_to(table[d : d + 1], (8, LANES))
            return carry

        lax.fori_loop(0, orb, one, 0, unroll=4)

    for t in owned:
        expand(coup_ref, own, left_coef, t)
    for copy in coup_copies:
        copy.wait()
    for t in owned:
        expand(call, chosen, right_coef, t)

    def dress(t, read, write):
        for e in range(rows):
            block = read(e)
            if block.shape[0] < LANES:
                block = jnp.concatenate([block, jnp.zeros((LANES - block.shape[0], width), jnp.float32)], axis=0)
            xt[e * width : (e + 1) * width, :] = jnp.transpose(block)

        def times_right(pair, carry):
            first = pair * 2
            held = [
                jnp.stack([xt[pl.ds((first + k) * orb + d, 8, stride=cells), :] for d in range(orb)])
                for k in range(2)
            ]
            for f in range(orb):
                factor = right_coef[t, f * orb : (f + 1) * orb]
                for k in range(2):
                    mid[f * orb + first + k] = jnp.sum(factor * held[k], axis=0)
            return carry

        lax.fori_loop(0, orb // 2, times_right, 0)

        def times_left(pair, carry):
            first = pair * 2
            held = [mid[pl.ds((first + k) * orb, orb)] for k in range(2)]
            for a in range(orb):
                factor = left_coef[t, a * orb : (a + 1) * orb]
                for k in range(2):
                    ot[pl.ds(a * orb + first + k, 8, stride=cells), :] = jnp.sum(factor * held[k], axis=0)
            return carry

        lax.fori_loop(0, orb // 2, times_left, 0)

        for e in range(rows):
            write(e, jnp.transpose(ot[e * width : (e + 1) * width, :]))

    def filtered(e, start, count):
        total = None
        for step, factor in weights:
            term = gbuf[e + step, pl.ds(start, count)].reshape(count * atoms, width) * factor
            total = term if total is None else total + term
        return total

    def receive_packed(t):
        first, count = packs[t]
        receive(len(pieces) + t)

        def unpack(m, carry):
            for row in range(2 * OFF):
                piece = arrived[row, m]
                target = row if row < OFF else rows + row
                for k in range(groups):
                    gbuf[target, m * groups + k, :, full:] = piece[:, k * rest : (k + 1) * rest]
            return carry

        lax.fori_loop(first, first + count, unpack, 0)

    for t in owned:
        start, count = spans[t]

        def write(e, block):
            gbuf[OFF + e, start : start + count] = block[: count * atoms].reshape(count, atoms, width)

        dress(t, lambda e: gbuf[OFF + e, start : start + count].reshape(count * atoms, width), write)
        for p in held_by[t]:
            send(p)
        send_packed(t)

    forward(0)
    for t in raw:
        expand(coup_ref, own, left_coef, t)
        expand(call, chosen, right_coef, t)

    for t in raw:
        start, count = spans[t]

        def write(e, block):
            out_ref[e, start : start + count] = block[: count * atoms].reshape(count, atoms, width)

        for p in level:
            if p > 0 and (p in held_by[t] or p == len(pieces) + t):
                forward(p)
        for p in held_by[t]:
            receive(p)
        receive_packed(t)
        dress(t, lambda e: filtered(e, start, count), write)

    for t in owned:
        receive_packed(t)
        for p in held_by[t]:
            start, count = pieces[p]
            receive(p)
            for e in range(rows):
                out_ref[e, start : start + count] = filtered(e, start, count).reshape(count, atoms, width)

    for p in range(len(pieces) + tiles):

        @pl.when(has_right)
        def _():
            halo(p, True).wait_send()

        @pl.when(has_left)
        def _():
            halo(p, False).wait_send()

    for p in level:

        @pl.when(jnp.logical_and(odd, via_left >= level[p]))
        def _():
            passed_on(p, False).wait_send()

        @pl.when(jnp.logical_and(even, via_right >= level[p]))
        def _():
            passed_on(p, True).wait_send()


def local(energy_count, atom_count, green_blocks, coupling, neighbours, freq_offset, emit_weight, absorb_weight):
    rows, atoms, nbrs, width = green_blocks.shape
    orb = coupling.shape[1]
    left_over = LANES // (width % LANES)
    spans = tile_spans(nbrs, LANES // atoms, left_over)
    tiles = len(spans)
    padded = tiles * LANES // atoms
    hbm = pl.BlockSpec(memory_space=pltpu.HBM)
    piece_count = tiles + 1
    f32 = jnp.float32
    result = pl.pallas_call(
        functools.partial(kernel, energy_count, atom_count),
        out_shape=pltpu.VMEM((rows, nbrs, atoms, width), f32),
        in_specs=[hbm] * 6,
        out_specs=pl.BlockSpec(memory_space=pltpu.VMEM),
        scratch_shapes=[
            pltpu.VMEM((orb, atoms, orb), f32),
            pltpu.VMEM((atoms, nbrs), jnp.int32),
            pltpu.VMEM((1, freq_offset.shape[0]), jnp.int32),
            pltpu.VMEM((1, freq_offset.shape[0]), f32),
            pltpu.VMEM((1, freq_offset.shape[0]), f32),
            pltpu.VMEM((rows + 2 * OFF, padded, atoms, width), f32),
            pltpu.VMEM((rows, -(-nbrs // left_over), atoms, LANES), f32),
            pltpu.VMEM((2 * OFF, -(-nbrs // left_over), atoms, LANES), f32),
            pltpu.VMEM((OFF, spans[-1][0], atoms, width // LANES * LANES), f32),
            pltpu.VMEM((OFF, spans[-1][0] // left_over, atoms, LANES), f32),
            pltpu.VMEM((orb, atoms * atom_count, orb), f32),
            pltpu.VMEM((tiles, orb * orb, 8, LANES), f32),
            pltpu.VMEM((tiles, orb * orb, 8, LANES), f32),
            pltpu.VMEM((rows * width, LANES), f32),
            pltpu.VMEM((orb * orb, 8, LANES), f32),
            pltpu.VMEM((rows * width, LANES), f32),
            pltpu.SemaphoreType.DMA((6,)),
            pltpu.SemaphoreType.DMA((2, piece_count + tiles)),
            pltpu.SemaphoreType.DMA((2, piece_count + tiles)),
            pltpu.SemaphoreType.DMA((piece_count + tiles,)),
            pltpu.SemaphoreType.DMA((piece_count + tiles,)),
            pltpu.SemaphoreType.DMA((max(atom_count - 1, 1),)),
            pltpu.SemaphoreType.DMA((max(atom_count - 1, 1),)),
        ],
        compiler_params=pltpu.CompilerParams(
            collective_id=0, has_side_effects=True, vmem_limit_bytes=48 * 1024 * 1024
        ),
    )(
        *(
            pltpu.with_memory_space_constraint(operand, pltpu.HBM)
            for operand in (
                jnp.transpose(green_blocks, (0, 2, 1, 3)),
                jnp.transpose(coupling, (1, 0, 2)),
                neighbours,
                freq_offset.reshape(1, -1),
                emit_weight.reshape(1, -1),
                absorb_weight.reshape(1, -1),
            )
        )
    )
    return jnp.transpose(result, (0, 2, 1, 3))


def solution(mesh):
    placed = (
        P("energy", "atom", None, None),
        P("atom", None, None),
        P("atom", None),
        P(),
        P(),
        P(),
    )
    return jax.shard_map(
        functools.partial(local, mesh.shape["energy"], mesh.shape["atom"]),
        mesh=mesh,
        in_specs=placed,
        out_specs=P("energy", "atom", None, None),
        check_vma=False,
    )
```

```python
import functools

import jax
import jax.numpy as jnp
from jax import lax
from jax.experimental import pallas as pl
from jax.experimental.pallas import tpu as pltpu
from jax.sharding import PartitionSpec as P

OFF = 2
QUARTERS = 4
LANES = 128
MESH = pl.DeviceIdType.MESH


def tile_spans(nbrs, per_tile, groups):
    second = (nbrs - per_tile) // 2 // groups * groups
    spans = [(0, per_tile), (per_tile, second), (per_tile + second, nbrs - per_tile - second)]
    assert 0 < second and spans[2][1] <= per_tile
    return spans


def kernel(
    energy_count,
    atom_count,
    x_ref,
    coup_hbm,
    nbr_hbm,
    freq_hbm,
    emit_hbm,
    absorb_hbm,
    out_ref,
    coup_ref,
    nbr_ref,
    freq_ref,
    emit_ref,
    absorb_ref,
    gbuf,
    packed,
    arrived,
    relay,
    relay_packed,
    call,
    right_coef,
    left_coef,
    xt,
    mid,
    ot,
    load_sem,
    halo_send,
    halo_recv,
    relay_send,
    relay_recv,
    coup_send,
    coup_recv,
):
    rows, nbrs, atoms, width = x_ref.shape
    orb = coup_hbm.shape[0]
    cells = orb * orb
    per_tile = LANES // atoms
    spans = tile_spans(nbrs, per_tile, LANES // (width % LANES))
    tiles = len(spans)
    full = width // LANES * LANES
    rest = width - full
    groups = LANES // rest
    packs = [(start // groups, -(-(start + count) // groups) - start // groups) for start, count in spans]
    early = (spans[0][1] + 2) // 2
    pieces = [(0, early), (early, spans[0][1] - early)] + spans[1:]
    held_by = {t: [p for p, (start, _) in enumerate(pieces) if spans[t][0] <= start < sum(spans[t])] for t in range(tiles)}
    level = {0: 1, 2: 2, len(pieces) + 1: 2, 1: 3, len(pieces): 3}
    raw = list(range(tiles - 1))[::-1]
    owned = [tiles - 1]
    all_atoms = atoms * atom_count

    me_e = lax.axis_index("energy")
    me_a = lax.axis_index("atom")
    has_left = me_e > 0
    has_right = me_e < energy_count - 1

    barrier = pltpu.get_barrier_semaphore()

    def greet(e, a):
        pl.semaphore_signal(barrier, inc=1, device_id=(e, a), device_id_type=MESH)

    @pl.when(has_left)
    def _():
        greet(me_e - 1, me_a)

    @pl.when(has_right)
    def _():
        greet(me_e + 1, me_a)

    @pl.when(me_e > 1)
    def _():
        greet(me_e - 2, me_a)

    @pl.when(me_e < energy_count - 2)
    def _():
        greet(me_e + 2, me_a)

    partners = [lax.rem(me_a + k, atom_count) for k in range(1, atom_count)]
    for partner in partners:
        greet(me_e, partner)
    loads = []
    for k, (src, dst) in enumerate(
        [
            (x_ref, gbuf.at[pl.ds(OFF, rows), pl.ds(0, nbrs)]),
            (coup_hbm, coup_ref),
            (nbr_hbm, nbr_ref),
            (freq_hbm, freq_ref),
            (emit_hbm, emit_ref),
            (absorb_hbm, absorb_ref),
        ]
    ):
        copy = pltpu.make_async_copy(src, dst, load_sem.at[k])
        copy.start()
        loads.append(copy)

    for copy in loads[1:]:
        copy.wait()
    freq = freq_ref[...]

    def weight(ref, step):
        return jnp.sum(jnp.where(freq == step, ref[...], 0.0), axis=1, keepdims=True)

    weights = [
        (0, weight(emit_ref, 2)),
        (1, weight(emit_ref, 1)),
        (3, weight(absorb_ref, 1)),
        (4, weight(absorb_ref, 2)),
    ]

    lanes = tiles * LANES
    slot = lax.broadcasted_iota(jnp.int32, (nbrs, lanes), 0)
    pair = lax.broadcasted_iota(jnp.int32, (nbrs, lanes), 1)
    listed_slot = pair // atoms
    for t in range(1, tiles):
        move = spans[t][0] - t * per_tile
        listed_slot = jnp.where(pair // LANES == t, pair // atoms + move, listed_slot)
    spread = jnp.where(listed_slot == slot, 1.0, 0.0).astype(jnp.float32)
    listed = jnp.dot(
        nbr_ref[...].astype(jnp.float32), spread, preferred_element_type=jnp.float32, precision=lax.Precision.HIGHEST
    )
    atom_row = lax.broadcasted_iota(jnp.int32, (atoms, lanes), 0)
    atom_pair = lax.broadcasted_iota(jnp.int32, (atoms, lanes), 1)
    own = jnp.where(atom_pair % atoms == atom_row, 1.0, 0.0).astype(jnp.float32)
    index = jnp.sum(listed * own, axis=0, keepdims=True)
    ids = lax.broadcasted_iota(jnp.int32, (all_atoms, lanes), 0).astype(jnp.float32)
    chosen = jnp.where(ids == index, 1.0, 0.0).astype(jnp.float32)

    outer = jnp.logical_or(me_e == 0, me_e == energy_count - 1)
    beside = jnp.logical_or(me_e == 1, me_e == energy_count - 2)

    @pl.when(outer)
    def _():
        pl.semaphore_wait(barrier, atom_count + 1)

    @pl.when(beside)
    def _():
        pl.semaphore_wait(barrier, atom_count + 2)

    @pl.when(jnp.logical_not(jnp.logical_or(outer, beside)))
    def _():
        pl.semaphore_wait(barrier, atom_count + 3)

    def own_rows(p, row):
        start, count = pieces[p]
        ref, row = (x_ref, row) if start < spans[-1][0] else (gbuf, row + OFF)
        return ref.at[pl.ds(row, OFF), pl.ds(start, count), :, pl.ds(0, full)]

    def halo(p, to_right):
        src_row, dst_row, side = (rows - OFF, 0, 0) if to_right else (0, rows + OFF, 1)
        if p >= len(pieces):
            first, count = packs[p - len(pieces)]
            src = packed.at[pl.ds(src_row, OFF), pl.ds(first, count)]
            dst = arrived.at[pl.ds(side * OFF, OFF), pl.ds(first, count)]
        else:
            start, count = pieces[p]
            src = own_rows(p, src_row)
            dst = gbuf.at[pl.ds(dst_row, OFF), pl.ds(start, count), :, pl.ds(0, full)]
        return pltpu.make_async_remote_copy(
            src_ref=src,
            dst_ref=dst,
            send_sem=halo_send.at[side, p],
            recv_sem=halo_recv.at[side, p],
            device_id=(me_e + 1 if to_right else me_e - 1, me_a),
            device_id_type=MESH,
        )

    pairs = energy_count // 2
    mine = lax.div(me_e, 2)
    odd = lax.rem(me_e, 2) == 1
    even = lax.rem(me_e, 2) == 0
    via_right = lax.div(QUARTERS * (pairs - 1 - mine), pairs)
    via_left = lax.div(QUARTERS * mine, pairs)

    def ends_of(p, to_right):
        src_row, dst_row, side = (rows - OFF, 0, 0) if to_right else (0, rows + OFF, 1)
        if p >= len(pieces):
            first, count = packs[p - len(pieces)]
            src = packed.at[pl.ds(src_row, OFF), pl.ds(first, count)]
            dst = arrived.at[pl.ds(side * OFF, OFF), pl.ds(first, count)]
            return src, relay_packed.at[:, pl.ds(first, count)], dst, side
        start, count = pieces[p]
        dst = gbuf.at[pl.ds(dst_row, OFF), pl.ds(start, count), :, pl.ds(0, full)]
        return own_rows(p, src_row), relay.at[:, pl.ds(start, count)], dst, side

    def detour(p, to_right):
        src, middle, _, side = ends_of(p, to_right)
        return pltpu.make_async_remote_copy(
            src_ref=src,
            dst_ref=middle,
            send_sem=halo_send.at[side, p],
            recv_sem=relay_recv.at[p],
            device_id=(me_e - 1 if to_right else me_e + 1, me_a),
            device_id_type=MESH,
        )

    def passed_on(p, to_right):
        _, middle, dst, side = ends_of(p, to_right)
        return pltpu.make_async_remote_copy(
            src_ref=middle,
            dst_ref=dst,
            send_sem=relay_send.at[p],
            recv_sem=halo_recv.at[side, p],
            device_id=(me_e + 2 if to_right else me_e - 2, me_a),
            device_id_type=MESH,
        )

    def send(p):
        if p in level:
            around_right = jnp.logical_and(odd, via_right >= level[p])
            around_left = jnp.logical_and(even, via_left >= level[p])

            @pl.when(around_right)
            def _():
                detour(p, True).start()

            @pl.when(around_left)
            def _():
                detour(p, False).start()

            straight_right = jnp.logical_and(has_right, jnp.logical_not(around_right))
            straight_left = jnp.logical_and(has_left, jnp.logical_not(around_left))
        else:
            straight_right, straight_left = has_right, has_left

        @pl.when(straight_right)
        def _():
            halo(p, True).start()

        @pl.when(straight_left)
        def _():
            halo(p, False).start()

    def forward(p):
        @pl.when(jnp.logical_and(odd, via_left >= level[p]))
        def _():
            detour(p, False).wait_recv()
            passed_on(p, False).start()

        @pl.when(jnp.logical_and(even, via_right >= level[p]))
        def _():
            detour(p, True).wait_recv()
            passed_on(p, True).start()

    def receive(p):
        @pl.when(has_left)
        def _():
            halo(p, True).wait_recv()

        @pl.when(has_right)
        def _():
            halo(p, False).wait_recv()

    coup_copies = []
    for k, partner in enumerate(partners):
        copy = pltpu.make_async_remote_copy(
            src_ref=coup_hbm,
            dst_ref=call.at[:, pl.ds(pl.multiple_of(me_a * atoms, atoms), atoms)],
            send_sem=coup_send.at[k],
            recv_sem=coup_recv.at[k],
            device_id=(me_e, partner),
            device_id_type=MESH,
        )
        copy.start()
        coup_copies.append(copy)

    for p in sorted((p for p in level if p < len(pieces)), key=level.get):
        send(p)

    loads[0].wait()
    gbuf[OFF : OFF + rows, nbrs:] = jnp.zeros((rows, gbuf.shape[1] - nbrs) + gbuf.shape[2:], jnp.float32)

    def send_packed(t):
        first, count = packs[t]

        def pack(m, carry):
            for e in range(rows):
                packed[e, m] = jnp.concatenate(
                    [gbuf[OFF + e, m * groups + k, :, full:] for k in range(groups)], axis=-1
                )
            return carry

        lax.fori_loop(first, first + count, pack, 0)
        send(len(pieces) + t)

    for t in raw:
        send_packed(t)

    call[:, pl.ds(pl.multiple_of(me_a * atoms, atoms), atoms), :] = coup_ref[...]

    @pl.when(jnp.logical_not(has_left))
    def _():
        gbuf[0:OFF] = jnp.zeros((OFF,) + gbuf.shape[1:], jnp.float32)
        arrived[0:OFF] = jnp.zeros((OFF,) + arrived.shape[1:], jnp.float32)

    @pl.when(jnp.logical_not(has_right))
    def _():
        gbuf[rows + OFF : rows + 2 * OFF] = jnp.zeros((OFF,) + gbuf.shape[1:], jnp.float32)
        arrived[OFF : 2 * OFF] = jnp.zeros((OFF,) + arrived.shape[1:], jnp.float32)

    def expand(source, select, target, t):
        def one(a, carry):
            table = lax.dot_general(
                source[a],
                select[:, t * LANES : (t + 1) * LANES],
                (((0,), (0,)), ((), ())),
                preferred_element_type=jnp.float32,
                precision=lax.Precision.HIGHEST,
            )
            for d in range(orb):
                target[t, a * orb + d] = jnp.broadcast_to(table[d : d + 1], (8, LANES))
            return carry

        lax.fori_loop(0, orb, one, 0, unroll=4)

    for t in owned:
        expand(coup_ref, own, left_coef, t)
    for copy in coup_copies:
        copy.wait()
    for t in owned:
        expand(call, chosen, right_coef, t)

    def dress(t, read, write):
        for e in range(rows):
            block = read(e)
            if block.shape[0] < LANES:
                block = jnp.concatenate([block, jnp.zeros((LANES - block.shape[0], width), jnp.float32)], axis=0)
            xt[e * width : (e + 1) * width, :] = jnp.transpose(block)

        def times_right(pair, carry):
            first = pair * 2
            held = [
                jnp.stack([xt[pl.ds((first + k) * orb + d, 8, stride=cells), :] for d in range(orb)])
                for k in range(2)
            ]
            for f in range(orb):
                factor = right_coef[t, f * orb : (f + 1) * orb]
                for k in range(2):
                    mid[f * orb + first + k] = jnp.sum(factor * held[k], axis=0)
            return carry

        lax.fori_loop(0, orb // 2, times_right, 0)

        def times_left(pair, carry):
            first = pair * 2
            held = [mid[pl.ds((first + k) * orb, orb)] for k in range(2)]
            for a in range(orb):
                factor = left_coef[t, a * orb : (a + 1) * orb]
                for k in range(2):
                    ot[pl.ds(a * orb + first + k, 8, stride=cells), :] = jnp.sum(factor * held[k], axis=0)
            return carry

        lax.fori_loop(0, orb // 2, times_left, 0)

        for e in range(rows):
            write(e, jnp.transpose(ot[e * width : (e + 1) * width, :]))

    def filtered(e, start, count):
        total = None
        for step, factor in weights:
            term = gbuf[e + step, pl.ds(start, count)].reshape(count * atoms, width) * factor
            total = term if total is None else total + term
        return total

    def receive_packed(t):
        first, count = packs[t]
        receive(len(pieces) + t)

        def unpack(m, carry):
            for row in range(2 * OFF):
                piece = arrived[row, m]
                target = row if row < OFF else rows + row
                for k in range(groups):
                    gbuf[target, m * groups + k, :, full:] = piece[:, k * rest : (k + 1) * rest]
            return carry

        lax.fori_loop(first, first + count, unpack, 0)

    for t in owned:
        start, count = spans[t]

        def write(e, block):
            gbuf[OFF + e, start : start + count] = block[: count * atoms].reshape(count, atoms, width)

        dress(t, lambda e: gbuf[OFF + e, start : start + count].reshape(count * atoms, width), write)
        for p in held_by[t]:
            send(p)
        send_packed(t)

    forward(0)
    for t in raw:
        expand(coup_ref, own, left_coef, t)
        expand(call, chosen, right_coef, t)

    for p in level:
        if p > 0:
            forward(p)

    for t in raw:
        start, count = spans[t]

        def write(e, block):
            out_ref[e, start : start + count] = block[: count * atoms].reshape(count, atoms, width)

        for p in held_by[t]:
            receive(p)
        receive_packed(t)
        dress(t, lambda e: filtered(e, start, count), write)

    for t in owned:
        receive_packed(t)
        for p in held_by[t]:
            start, count = pieces[p]
            receive(p)
            for e in range(rows):
                out_ref[e, start : start + count] = filtered(e, start, count).reshape(count, atoms, width)

    for p in range(len(pieces) + tiles):

        @pl.when(has_right)
        def _():
            halo(p, True).wait_send()

        @pl.when(has_left)
        def _():
            halo(p, False).wait_send()

    for p in level:

        @pl.when(jnp.logical_and(odd, via_left >= level[p]))
        def _():
            passed_on(p, False).wait_send()

        @pl.when(jnp.logical_and(even, via_right >= level[p]))
        def _():
            passed_on(p, True).wait_send()


def local(energy_count, atom_count, green_blocks, coupling, neighbours, freq_offset, emit_weight, absorb_weight):
    rows, atoms, nbrs, width = green_blocks.shape
    orb = coupling.shape[1]
    left_over = LANES // (width % LANES)
    spans = tile_spans(nbrs, LANES // atoms, left_over)
    tiles = len(spans)
    padded = tiles * LANES // atoms
    hbm = pl.BlockSpec(memory_space=pltpu.HBM)
    piece_count = tiles + 1
    f32 = jnp.float32
    result = pl.pallas_call(
        functools.partial(kernel, energy_count, atom_count),
        out_shape=pltpu.VMEM((rows, nbrs, atoms, width), f32),
        in_specs=[hbm] * 6,
        out_specs=pl.BlockSpec(memory_space=pltpu.VMEM),
        scratch_shapes=[
            pltpu.VMEM((orb, atoms, orb), f32),
            pltpu.VMEM((atoms, nbrs), jnp.int32),
            pltpu.VMEM((1, freq_offset.shape[0]), jnp.int32),
            pltpu.VMEM((1, freq_offset.shape[0]), f32),
            pltpu.VMEM((1, freq_offset.shape[0]), f32),
            pltpu.VMEM((rows + 2 * OFF, padded, atoms, width), f32),
            pltpu.VMEM((rows, -(-nbrs // left_over), atoms, LANES), f32),
            pltpu.VMEM((2 * OFF, -(-nbrs // left_over), atoms, LANES), f32),
            pltpu.VMEM((OFF, spans[-1][0], atoms, width // LANES * LANES), f32),
            pltpu.VMEM((OFF, spans[-1][0] // left_over, atoms, LANES), f32),
            pltpu.VMEM((orb, atoms * atom_count, orb), f32),
            pltpu.VMEM((tiles, orb * orb, 8, LANES), f32),
            pltpu.VMEM((tiles, orb * orb, 8, LANES), f32),
            pltpu.VMEM((rows * width, LANES), f32),
            pltpu.VMEM((orb * orb, 8, LANES), f32),
            pltpu.VMEM((rows * width, LANES), f32),
            pltpu.SemaphoreType.DMA((6,)),
            pltpu.SemaphoreType.DMA((2, piece_count + tiles)),
            pltpu.SemaphoreType.DMA((2, piece_count + tiles)),
            pltpu.SemaphoreType.DMA((piece_count + tiles,)),
            pltpu.SemaphoreType.DMA((piece_count + tiles,)),
            pltpu.SemaphoreType.DMA((max(atom_count - 1, 1),)),
            pltpu.SemaphoreType.DMA((max(atom_count - 1, 1),)),
        ],
        compiler_params=pltpu.CompilerParams(
            collective_id=0, has_side_effects=True, vmem_limit_bytes=48 * 1024 * 1024
        ),
    )(
        *(
            pltpu.with_memory_space_constraint(operand, pltpu.HBM)
            for operand in (
                jnp.transpose(green_blocks, (0, 2, 1, 3)),
                jnp.transpose(coupling, (1, 0, 2)),
                neighbours,
                freq_offset.reshape(1, -1),
                emit_weight.reshape(1, -1),
                absorb_weight.reshape(1, -1),
            )
        )
    )
    return jnp.transpose(result, (0, 2, 1, 3))


def solution(mesh):
    placed = (
        P("energy", "atom", None, None),
        P("atom", None, None),
        P("atom", None),
        P(),
        P(),
        P(),
    )
    return jax.shard_map(
        functools.partial(local, mesh.shape["energy"], mesh.shape["atom"]),
        mesh=mesh,
        in_specs=placed,
        out_specs=P("energy", "atom", None, None),
        check_vma=False,
    )
```
